256 devices in a mesh: dp: 16 (over z_lo, y), expert: 16 (over x, z_hi, core).
Axes of the slice: x: 4, y: 4, z: 8 (z_hi: 2, z_lo: 4; z = z_hi * 4 + z_lo), core: 2. Of those that a mesh axis runs over, the one named last changes fastest.
Arguments:
- values: bfloat16 [2048, 3072], P('expert', 'dp'), may hold values from -6 to 6
- exponents: int32 [2048, 24], P('expert'), may hold values from -2 to 2
- expert_ids: int32 [2048, 4], P('expert'), may hold values from 0 to 15, all different within a row; in each aligned block of 128 rows (0 to 127, 128 to 255, ...) at most 36 rows name the same one
- route_weights: bfloat16 [2048, 4], P('expert'), may hold values from 0.049804688 to 0.59765625
- cotangent: bfloat16 [2048, 3072], P('expert', 'dp'), may hold values from -2 to 2
- w_gate: bfloat16 [16, 5376, 3072], P('expert', 'dp'), may hold values from -0.109375 to 0.109375
- w_up: bfloat16 [16, 5376, 3072], P('expert', 'dp'), may hold values from -0.109375 to 0.109375
- w_down: bfloat16 [16, 5376, 3072], P('expert', 'dp'), may hold values from -0.078125 to 0.078125
Outputs:
- d_values: bfloat16 [2048, 3072], P('expert', 'dp')
- d_route_weights: bfloat16 [2048, 4], P('expert')
- grad_gate: bfloat16 [16, 5376, 3072], P('expert', 'dp')
- grad_up: bfloat16 [16, 5376, 3072], P('expert', 'dp')
- grad_down: bfloat16 [16, 5376, 3072], P('expert', 'dp')
The draws below stay inside these ranges and needn't reach their ends.
Inputs may be any that keep to these rules, and one draw needn't show every extreme that they name: `expert_ids`: each row names 4 different experts. Among the rows of one index of expert no expert is named more than 36 times, a bound that some block reaches.
All inputs are finite; a program needn't handle non-finite values.
Results may differ from the reference program's by a relative error of at most 0.024.
Values may be sent and summed in bfloat16 or wider, within the bound.
A program may use at most 128 MiB of HBM per device.

```python
import math
import jax
import jax.numpy as jnp
import numpy as np
from jax import lax

D = 3072
TOP = 4
FFW = 5376
TOK_DEV = 128
EXPERTS = 16
CAP = 36
TOKENS = 2048
N_DP = 16
N_EXPERT = 16


def plant(result, stream_key, smallest, largest):
    longest = result.shape.index(max(result.shape))
    spots = []
    for shift in (0, 1):
        where = [jax.random.randint(jax.random.fold_in(stream_key, axis), (), 0, length) for axis, length in enumerate(result.shape)]
        where[longest] = (where[longest] + shift) % result.shape[longest]
        spots.append(tuple(where))
    return result.at[spots[0]].set(smallest).at[spots[1]].set(largest)


def levels(stream_key, extent, shards, least, top_value):
    def one(axis_at, blocks):
        steps = jax.random.uniform(jax.random.fold_in(jax.random.fold_in(stream_key, 6), axis_at), (blocks,), jnp.float32, least / len(shards), top_value / len(shards))
        return jnp.repeat(jnp.exp(steps), extent[axis_at] // blocks).reshape((-1,) + (1,) * (len(extent) - axis_at - 1))

    factor_of = one(*shards[0])
    for cut in shards[1:]:
        factor_of = factor_of * one(*cut)
    return factor_of


def shared_out(own_key, own, number, rows, amount, top, most, lean):
    ranking = jax.random.permutation(own_key, amount)
    packed, ordinary = load_shares(amount, rows * top, most, lean, True), load_shares(amount, rows * top, most, lean, False)
    places = jnp.arange(amount)

    def named(lengths, offset_by):
        used = int((lengths > 0).sum())
        fixed = max(1, used // 4)
        shifted = fixed + (places - fixed + offset_by * (used - fixed)) % max(1, amount - fixed)
        return jnp.zeros((amount,), jnp.int32).at[ranking[jnp.where(places < fixed, places, shifted)]].set(jnp.asarray(lengths, jnp.int32))

    lengths = jnp.where(number % 4 == 0, named(packed, number // 4), named(ordinary, number - number // 4 - 1))
    mixed = jax.random.permutation(jax.random.fold_in(own, 3), amount)
    source_of, receiver = mixed[0:amount // 2 * 2:2], mixed[1:amount // 2 * 2:2]
    margin = jnp.minimum(lengths[source_of] - 1, most - lengths[receiver]) // 2
    margin = jnp.where((source_of == ranking[0]) | (receiver == ranking[0]) | (lengths[receiver] == 0), 0, jnp.maximum(margin, 0))
    shifted = jax.random.randint(jax.random.fold_in(own, 4), (amount // 2,), 0, 1 << 20) % (margin + 1)
    lengths = lengths.at[source_of].add(-shifted).at[receiver].add(shifted)
    labels = jnp.searchsorted(jnp.cumsum(lengths), jnp.arange(rows * top), side="right").astype(jnp.int32)
    listing = labels.reshape(top, rows).T
    listing = listing[jax.random.permutation(jax.random.fold_in(own, 1), rows)]
    offset_by = jax.random.randint(jax.random.fold_in(own, 2), (rows, 1), 0, top)
    return jnp.take_along_axis(listing, (jnp.arange(top)[None, :] + offset_by) % top, axis=1)


def load_shares(count, total, reach, skew, full):
    loads = [(1 << 20) // math.isqrt(grade ** skew) + 1 for grade in range(1, count + 1)]
    largest = reach if full else min(reach, max(-(-total // count), total * loads[0] // sum(loads)))
    least = 1 if total - largest >= count - 1 else 0
    given, rest = [largest] + [least] * (count - 1), total - largest - least * (count - 1)
    while rest > 0:
        free = [i for i in range(1, count) if given[i] < largest] or [i for i in range(1, count) if given[i] < reach]
        mass, remaining = sum([loads[i] for i in free]), rest
        for i in free:
            addition = min(reach - given[i], max(1, remaining * loads[i] // mass), rest)
            given[i] = given[i] + addition
            rest = rest - addition
    return np.array(given)


def normal_values(own_key, dims, deviation, bound, cuts=(), held_as=jnp.bfloat16):
    entries = jax.random.normal(own_key, dims, jnp.float32) * deviation
    if len(cuts) > 0:
        entries = levels(own_key, dims, cuts, -0.22, 0.18) * entries
    return jnp.clip(entries, min=-bound, max=bound).astype(held_as)


def setup_inputs(seed: int = 0) -> dict:
    key_of = jax.random.split(jax.random.key(seed), 9)
    values = normal_values(key_of[0], (TOKENS, D), 1.0, 6.0, ((0, 16), (1, 16)))
    exponents = plant(jax.random.randint(key_of[1], (TOKENS, D // 128), -2, 3), jax.random.fold_in(key_of[1], 1), -2, 2).astype(jnp.int32)
    expert_ids_keys = jax.random.split(jax.random.fold_in(key_of[2], 1), TOKENS // TOK_DEV)
    expert_ids_turns = jax.random.permutation(jax.random.fold_in(key_of[2], 3), TOKENS // TOK_DEV)
    expert_ids = jax.vmap(lambda own, number: shared_out(jax.random.fold_in(key_of[2], 2), own, number, TOK_DEV, EXPERTS, TOP, CAP, 2))(expert_ids_keys, expert_ids_turns).reshape((TOKENS, TOP))
    route_weights = jnp.clip(0.049804688 + 0.54785156 * jax.random.uniform(key_of[3], (TOKENS, TOP), jnp.float32) ** levels(key_of[3], (TOKENS, TOP), ((0, 16),), -0.2, 0.2), 0.049804688, 0.59765625).astype(jnp.bfloat16)
    cotangent = normal_values(key_of[4], (TOKENS, D), 0.125, 2.0, ((0, 16), (1, 16)))
    w_gate = normal_values(key_of[5], (EXPERTS, FFW, D), D ** -0.5, 0.109375, ((0, 16), (1, 16)))
    w_up = normal_values(key_of[6], (EXPERTS, FFW, D), D ** -0.5, 0.109375, ((0, 16), (1, 16)))
    w_down = normal_values(key_of[7], (EXPERTS, FFW, D), FFW ** -0.5, 0.078125, ((0, 16), (1, 16)))
    return {"values": values, "exponents": exponents, "expert_ids": expert_ids, "route_weights": route_weights, "cotangent": cotangent, "w_gate": w_gate, "w_up": w_up, "w_down": w_down}


def expert_pass(inputs, out_cot, probs, gate_w, up_w, down_w):
    gate = jnp.dot(inputs, gate_w.T, preferred_element_type=jnp.float32)
    upper = jnp.dot(inputs, up_w.T, preferred_element_type=jnp.float32)
    sigmoid_gate = jax.nn.sigmoid(gate)
    swished = gate * sigmoid_gate
    hidden = (swished * upper).astype(jnp.bfloat16)
    output = jnp.dot(hidden, down_w, preferred_element_type=jnp.float32)
    prob_grad = jnp.sum(output * out_cot.astype(jnp.float32), axis=1).astype(jnp.bfloat16)
    scaled_cot = (probs.astype(jnp.float32)[:, None] * out_cot.astype(jnp.float32)).astype(jnp.bfloat16)
    hidden_grad = jnp.dot(scaled_cot, down_w.T, preferred_element_type=jnp.float32)
    gate_grad = (hidden_grad * upper * sigmoid_gate * (1.0 + gate * (1.0 - sigmoid_gate))).astype(jnp.bfloat16)
    upper_grad = (hidden_grad * swished).astype(jnp.bfloat16)
    block_width = gate_w.shape[0] // N_DP
    total = jnp.zeros((inputs.shape[0], inputs.shape[1]), jnp.float32)
    for block in range(N_DP):
        low = block * block_width
        high = low + block_width
        block_part = (jnp.dot(gate_grad[:, low:high], gate_w[low:high], preferred_element_type=jnp.float32)
                      + jnp.dot(upper_grad[:, low:high], up_w[low:high], preferred_element_type=jnp.float32)).astype(jnp.bfloat16)
        block_part = lax.optimization_barrier(block_part)
        total = total + block_part.astype(jnp.float32)
    input_grad = total.astype(jnp.bfloat16)
    weight_gate = jnp.dot(gate_grad.T, inputs, preferred_element_type=jnp.float32)
    weight_up = jnp.dot(upper_grad.T, inputs, preferred_element_type=jnp.float32)
    weight_down = jnp.dot(hidden.T, scaled_cot, preferred_element_type=jnp.float32)
    return input_grad, prob_grad, weight_gate, weight_up, weight_down


def reference(values, exponents, expert_ids, route_weights, cotangent, w_gate, w_up, w_down):
    count = values.shape[0]
    blocks = exponents.shape[1]
    scales = jnp.exp2(exponents.astype(jnp.float32))
    inputs = (values.astype(jnp.float32).reshape(count, blocks, -1) * scales[:, :, None]).reshape(count, -1).astype(jnp.bfloat16)
    flat_ids = expert_ids.reshape(-1)
    flat_probs = route_weights.reshape(-1)
    limit = N_EXPERT * CAP

    def visit(carry, expert):
        grad_rows, prob_rows = carry
        routed = flat_ids == expert
        picked = jnp.nonzero(routed, size=limit, fill_value=0)[0].astype(jnp.int32)
        live = jnp.arange(limit, dtype=jnp.int32) < jnp.sum(routed.astype(jnp.int32))
        owner = (picked // TOP).astype(jnp.int32)
        rows = jnp.where(live[:, None], inputs[owner], jnp.zeros((), jnp.bfloat16))
        cot_rows = jnp.where(live[:, None], cotangent[owner], jnp.zeros((), jnp.bfloat16))
        prob_sel = jnp.where(live, flat_probs[picked], jnp.zeros((), jnp.bfloat16))
        results = expert_pass(rows, cot_rows, prob_sel, w_gate[expert], w_up[expert], w_down[expert])
        grad_rows = grad_rows.at[owner].add(jnp.where(live[:, None], results[0].astype(jnp.float32), 0.0))
        prob_rows = prob_rows.at[picked].add(jnp.where(live, results[1].astype(jnp.float32), 0.0))
        return (grad_rows, prob_rows), (results[2], results[3], results[4])

    start = (jnp.zeros(values.shape, jnp.float32), jnp.zeros(flat_ids.shape, jnp.float32))
    (grad_rows, prob_rows), grads = lax.scan(visit, start, jnp.arange(EXPERTS, dtype=jnp.int32))
    d_values = (grad_rows.reshape(count, blocks, -1) * scales[:, :, None]).reshape(count, -1).astype(jnp.bfloat16)
    d_route = prob_rows.reshape(expert_ids.shape).astype(jnp.bfloat16)
    return (d_values, d_route, grads[0].astype(jnp.bfloat16), grads[1].astype(jnp.bfloat16), grads[2].astype(jnp.bfloat16))
```

```python
import functools

import jax
import jax.numpy as jnp
from jax import lax
from jax.experimental import pallas as pl
from jax.experimental.pallas import tpu as pltpu
from jax.sharding import PartitionSpec as P

MESH = pl.DeviceIdType.MESH

SLOT = 48
CAP = 36
TOK = 128
BLK = 384
ZCOL = 2 * BLK
HID = 336
HPAD = 384
FEAT = 3072
ROWS = 16 * CAP
HALF = ROWS // 2
QTR = HALF // 2


def nt(left, right):
    return lax.dot_general(left, right, (((1,), (1,)), ((), ())), preferred_element_type=jnp.float32)


def tn(left, right):
    return lax.dot_general(left, right, (((0,), (0,)), ((), ())), preferred_element_type=jnp.float32)


def nn(left, right):
    return jnp.dot(left, right, preferred_element_type=jnp.float32)


def kernel(
    mine, give, pick_w, pick, squeeze, spread, row_of, slot_of, wg, wu, wd,
    res, back, gg_out, gu_out, gd_out,
    got, sendb, recvb, xs, w2, w3, acc_gu, acc_h, hid, hidden, hid_t, hidden_t, prob, part,
    diag, dsum, ybuf, zsend, zrecv, retsend, retrecv, pbuf, py, pz, ptot, ogu, ogd,
    swap_sem, disp_send, disp_recv, w_sem, gz_send, gz_recv, gy_send, gy_recv, gd_send, gd_recv,
    rd_send, rd_recv, ro_send, ro_recv, rs_send, rs_recv, rz_send, rz_recv,
    ret_send, ret_recv, fin_sem, p_send, p_recv, pb_send, pb_recv, out_sem,
):
    d = lax.axis_index("dp")
    e = lax.axis_index("expert")
    y, zl = lax.rem(d, 4), d // 4
    par, sub = lax.rem(y, 2), y // 2
    x, zh, c = e // 4, lax.rem(e // 2, 2), lax.rem(e, 2)
    rank = zh * 8 + x * 2 + c

    def at_y(step):
        return (zl * 4 + lax.rem(y + step + 4, 4), e)

    def at_z(z):
        return (z * 4 + y, e)

    def expert_of(r):
        return lax.rem(r, 8) // 2 * 4 + r // 8 * 2 + lax.rem(r, 2)

    def remote(src, dst, ssem, rsem, dev):
        return pltpu.make_async_remote_copy(src, dst, ssem, rsem, device_id=dev, device_id_type=MESH)

    bar = pltpu.get_barrier_semaphore()
    for step in (1, 2, 3):
        pl.semaphore_signal(bar, inc=1, device_id=at_y(step), device_id_type=MESH)
        pl.semaphore_signal(bar, inc=1, device_id=at_z(lax.rem(zl + step, 4)), device_id_type=MESH)
    for step in range(1, 16):
        pl.semaphore_signal(bar, inc=1, device_id=(d, lax.rem(e + step, 16)), device_id_type=MESH)

    loads = [
        pltpu.make_async_copy(wg, w2.at[pl.ds(0, HID)], w_sem.at[0]),
        pltpu.make_async_copy(wu, w2.at[pl.ds(HPAD, HID)], w_sem.at[1]),
        pltpu.make_async_copy(wd, w3.at[pl.ds(0, HID)], w_sem.at[2]),
    ]
    for load in loads:
        load.start()
    pl.semaphore_wait(bar, 21)

    partner = (zl * 4 + y + 1 - 2 * par, e)
    swap = remote(give, got, swap_sem.at[0], swap_sem.at[1], partner)
    swap.start()
    w2[pl.ds(HID, HPAD - HID), :] = jnp.zeros((HPAD - HID, FEAT), jnp.bfloat16)
    w2[pl.ds(HPAD + HID, HPAD - HID), :] = jnp.zeros((HPAD - HID, FEAT), jnp.bfloat16)
    w3[pl.ds(HID, HPAD - HID), :] = jnp.zeros((HPAD - HID, FEAT), jnp.bfloat16)
    acc_gu[...] = jnp.zeros_like(acc_gu)
    acc_h[...] = jnp.zeros_like(acc_h)
    swap.wait()
    both = mine[...] + got[...]
    picked = nn(pick_w[...], both).astype(jnp.bfloat16)
    for r in range(16):
        sendb[r] = picked[r * SLOT : (r + 1) * SLOT]

    def dispatch(r):
        return remote(sendb.at[r], recvb.at[rank], disp_send.at[r], disp_recv.at[rank], (d, expert_of(r)))

    def arrival(r):
        return remote(sendb.at[rank], recvb.at[r], disp_send.at[rank], disp_recv.at[r], (d, expert_of(r)))

    @pl.loop(0, 16)
    def _(i):
        r = lax.rem(i + zh * 8, 16)

        @pl.when(r != rank)
        def _():
            dispatch(r).start()

    recvb[rank] = sendb[rank]

    def block(ref, z, yy, row, rows):
        return ref.at[lax.rem(yy, 2), pl.ds(pl.multiple_of(row, 16), rows),
                      pl.ds(pl.multiple_of(z * ZCOL + yy // 2 * BLK, 128), BLK)]

    def z_copy(h, j):
        ref = block(xs, zl, y, h * HALF, HALF)
        return remote(ref, ref, gz_send.at[h, j], gz_recv.at[h, j], at_z(lax.rem(zl + j, 4)))

    def z_arrival(h, j):
        ref = block(xs, lax.rem(zl - j + 4, 4), y, h * HALF, HALF)
        return remote(ref, ref, gz_send.at[h, j], gz_recv.at[h, j], at_z(lax.rem(zl + j, 4)))

    def take_half(h):
        @pl.loop(0, 8)
        def _(i):
            r = h * 8 + i

            @pl.when(r != rank)
            def _():
                arrival(r).wait_recv()

        slabs = recvb[pl.ds(h * 8, 8)].reshape(8 * SLOT, BLK)
        rows = nn(squeeze[...], slabs).astype(jnp.bfloat16)
        xs[par, pl.ds(pl.multiple_of(h * HALF, 16), HALF),
           pl.ds(pl.multiple_of(zl * ZCOL + sub * BLK, 128), BLK)] = rows
        for j in (1, 2, 3):
            z_copy(h, j).start()

    def chunk(s):
        i, j = s // 4, lax.rem(s, 4)
        h = lax.rem(zh + i, 2)
        return h, j, lax.rem(zl - j + 4, 4)

    left, right = lax.rem(y + 3, 4), lax.rem(y + 1, 4)
    across = lax.rem(y + 2, 4)

    def y_copy(s, way):
        h, j, z = chunk(s)
        ref = block(xs, z, y, h * HALF, HALF)
        return remote(ref, ref, gy_send.at[s, way], gy_recv.at[s, way], at_y(1 if way == 0 else 3))

    def y_arrival(s, way):
        h, j, z = chunk(s)
        ref = block(xs, z, left if way == 0 else right, h * HALF, HALF)
        return remote(ref, ref, gy_send.at[s, way], gy_recv.at[s, way], at_y(1 if way == 0 else 3))

    def d_copy(s, way):
        h, j, z = chunk(s)
        ref = block(xs, z, left if way == 0 else right, h * HALF + way * QTR, QTR)
        return remote(ref, ref, gd_send.at[s, way], gd_recv.at[s, way], at_y(1 if way == 0 else 3))

    def d_arrival(s, way):
        h, j, z = chunk(s)
        ref = block(xs, z, across, h * HALF + way * QTR, QTR)
        return remote(ref, ref, gd_send.at[s, way], gd_recv.at[s, way], at_y(1 if way == 0 else 3))

    take_half(zh)
    y_copy(0, 0).start()
    y_copy(0, 1).start()
    for load in loads:
        load.wait()

    @pl.loop(0, 9)
    def _(s):
        @pl.when(s == 2)
        def _():
            take_half(1 - zh)

        @pl.when(s < 7)
        def _():
            h, j, z = chunk(s + 1)

            @pl.when(j > 0)
            def _():
                z_arrival(h, j).wait_recv()

            y_copy(s + 1, 0).start()
            y_copy(s + 1, 1).start()

        @pl.when(s < 8)
        def _():
            for way in (0, 1):
                y_arrival(s, way).wait_recv()
                d_copy(s, way).start()

        @pl.when(s > 0)
        def _():
            for way in (0, 1):
                d_arrival(s - 1, way).wait_recv()
            h, j, z = chunk(s - 1)
            rows = pl.ds(pl.multiple_of(h * HALF, 16), HALF)
            cols = pl.ds(pl.multiple_of(z * ZCOL, 128), ZCOL)
            acc_gu[rows, :] += nt(xs[0, rows, cols], w2[:, cols])
            acc_h[rows, :] += nt(xs[1, rows, cols], w3[:, cols])

            @pl.when(j == 3)
            def _():
                @pl.loop(0, HALF // 32)
                def _(b):
                    part_rows = pl.ds(pl.multiple_of(h * HALF + b * 32, 16), 32)
                    gate = acc_gu[part_rows, pl.ds(0, HPAD)]
                    upper = acc_gu[part_rows, pl.ds(HPAD, HPAD)]
                    grad = acc_h[part_rows, :]
                    sig = jax.nn.sigmoid(gate)
                    swished = gate * sig
                    act = (swished * upper).astype(jnp.bfloat16)
                    hidden[part_rows, :] = act
                    hid[part_rows, pl.ds(0, HPAD)] = (
                        grad * upper * sig * (1.0 + gate * (1.0 - sig))
                    ).astype(jnp.bfloat16)
                    hid[part_rows, pl.ds(HPAD, HPAD)] = (grad * swished).astype(jnp.bfloat16)
                    total = jnp.sum(act.astype(jnp.float32) * grad, axis=1, keepdims=True)
                    prob[part_rows, :] = jnp.broadcast_to(total, (32, 128))

    for h in (0, 1):
        pbuf[pl.ds(h * 8, 8), :] = jnp.dot(
            row_of[...], prob[pl.ds(h * HALF, HALF), :] * slot_of[...],
            precision=lax.Precision.HIGHEST, preferred_element_type=jnp.float32,
        )

    def p_y(j):
        return remote(pbuf, py.at[j - 1], p_send.at[j - 1], p_recv.at[j - 1], at_y(j))

    def p_z(j):
        return remote(pz.at[3], pz.at[j - 1], p_send.at[2 + j], p_recv.at[2 + j], at_z(lax.rem(zl + j, 4)))

    def p_b(step):
        return remote(ptot, back.at[rank], pb_send.at[step], pb_recv.at[rank],
                      (d, lax.rem(e + step, 16)))

    for j in (1, 2, 3):
        p_y(j).start()

    def piece(yy, z, row, rows):
        return (pl.ds(pl.multiple_of(lax.rem(yy, 2) * HALF + row, 16), rows),
                pl.ds(pl.multiple_of(z * ZCOL + yy // 2 * BLK, 128), BLK))

    def zdest(q):
        return lax.rem(zl + 1 + q, 4)

    def diag_copy(q, way):
        src = part.at[piece(across, zdest(q), way * QTR, QTR)]
        return remote(src, diag.at[q, way], rd_send.at[q, way], rd_recv.at[q, way], at_y(1 if way == 0 else 3))

    def own_copy(q, way):
        to = right if way == 0 else left
        src = part.at[piece(to, zdest(q), (1 - way) * QTR, QTR)]
        return remote(src, ybuf.at[q, way, 1 - way], ro_send.at[q, way], ro_recv.at[q, way], at_y(1 if way == 0 else 3))

    def sum_copy(q, way):
        return remote(dsum.at[q, way], ybuf.at[q, way, way], rs_send.at[q, way], rs_recv.at[q, way],
                      at_y(1 if way == 0 else 3))

    def zred_copy(q):
        return remote(zsend.at[q], zrecv.at[q], rz_send.at[q], rz_recv.at[q], at_z(zdest(q)))

    def make_part(q):
        cols = pl.ds(pl.multiple_of(zdest(q) * ZCOL, 128), ZCOL)
        part[:, cols] = nn(hid[...], w2[:, cols]).astype(jnp.bfloat16)
        for way in (0, 1):
            diag_copy(q, way).start()
        for way in (0, 1):
            own_copy(q, way).start()

    def out_copies(q):
        cols = pl.ds(pl.multiple_of(q * ZCOL, 128), ZCOL)
        return (
            pltpu.make_async_copy(ogu.at[pl.ds(0, HID), cols], gg_out.at[:, cols], out_sem.at[q, 0]),
            pltpu.make_async_copy(ogu.at[pl.ds(HPAD, HID), cols], gu_out.at[:, cols], out_sem.at[q, 1]),
            pltpu.make_async_copy(ogd.at[pl.ds(0, HID), cols], gd_out.at[:, cols], out_sem.at[q, 2]),
        )

    def weight_grads(q):
        cols = pl.ds(pl.multiple_of(q * ZCOL, 128), ZCOL)
        ogu[:, cols] = nn(hid_t[...], xs[0, :, cols]).astype(jnp.bfloat16)
        ogd[:, cols] = nn(hidden_t[...], xs[1, :, cols]).astype(jnp.bfloat16)
        for out in out_copies(q):
            out.start()

    def y_sum(q):
        for way in (0, 1):
            own_copy(q, way).wait_recv()
            sum_copy(q, way).wait_recv()
        own = part[piece(y, zdest(q), 0, HALF)].astype(jnp.float32)
        return own + (ybuf[q, 0].reshape(HALF, BLK).astype(jnp.float32)
                      + ybuf[q, 1].reshape(HALF, BLK).astype(jnp.float32))

    make_part(0)
    hid_t[...] = hid[...].T
    hidden_t[...] = hidden[...].T

    @pl.loop(0, 4)
    def _(q):
        @pl.when(q < 3)
        def _():
            make_part(q + 1)

        for way in (0, 1):
            diag_copy(q, way).wait_recv()
            to = right if way == 0 else left
            dsum[q, way] = (
                part[piece(to, zdest(q), way * QTR, QTR)].astype(jnp.float32)
                + diag[q, way].astype(jnp.float32)
            ).astype(jnp.bfloat16)
            sum_copy(q, way).start()

        weight_grads(q)

        @pl.when(q == 0)
        def _():
            for j in (1, 2, 3):
                p_y(j).wait_recv()
            pz[3] = pbuf[...] + py[0] + py[1] + py[2]
            for j in (1, 2, 3):
                p_z(j).start()

        @pl.when(q == 1)
        def _():
            for j in (1, 2, 3):
                p_z(j).wait_recv()
            ptot[...] = pz[0] + pz[1] + pz[2] + pz[3]
            back[rank] = ptot[...]

            @pl.loop(1, 16)
            def _(step):
                p_b(step).start()

        @pl.when(q > 0)
        def _():
            zsend[q - 1] = y_sum(q - 1).astype(jnp.bfloat16)
            zred_copy(q - 1).start()

    total = y_sum(3)
    for q in range(3):
        zred_copy(q).wait_recv()
        total += zrecv[q].astype(jnp.float32)
    slabs = nn(spread[...], total.astype(jnp.bfloat16)).astype(jnp.bfloat16)
    for i in range(8):
        retsend[i] = slabs[i * SLOT : (i + 1) * SLOT]

    def ret_copy(i):
        return remote(retsend.at[i], retrecv.at[rank], ret_send.at[i], ret_recv.at[rank],
                      (d, expert_of(par * 8 + i)))

    def ret_arrival(r):
        return remote(retsend.at[0], retrecv.at[r], ret_send.at[0], ret_recv.at[r], (d, expert_of(r)))

    @pl.loop(0, 8)
    def _(i):
        @pl.when(par * 8 + i != rank)
        def _():
            ret_copy(i).start()

    fin = remote(res, res, fin_sem.at[0], fin_sem.at[1], partner)

    @pl.when(zh == par)
    def _():
        retrecv[rank] = retsend[rank - par * 8]

        @pl.loop(0, 16)
        def _(r):
            @pl.when(r != rank)
            def _():
                ret_arrival(r).wait_recv()

        res[...] = tn(pick[...], retrecv[...].reshape(16 * SLOT, BLK)).astype(jnp.bfloat16)
        fin.start()
        fin.wait_send()

    @pl.when(zh != par)
    def _():
        fin.wait_recv()

    @pl.loop(0, 16)
    def _(r):
        @pl.when(r != rank)
        def _():
            dispatch(r).wait_send()
            remote(ptot, back.at[r], pb_send.at[0], pb_recv.at[r], (d, expert_of(r))).wait_recv()

    @pl.loop(1, 16)
    def _(step):
        p_b(step).wait_send()

    @pl.loop(0, 8)
    def _(i):
        @pl.when(par * 8 + i != rank)
        def _():
            ret_copy(i).wait_send()

    @pl.loop(0, 8)
    def _(s):
        for way in (0, 1):
            y_copy(s, way).wait_send()
            d_copy(s, way).wait_send()

    for j in (1, 2, 3):
        for h in (0, 1):
            z_copy(h, j).wait_send()
        p_y(j).wait_send()
        p_z(j).wait_send()

    @pl.loop(0, 4)
    def _(q):
        for way in (0, 1):
            diag_copy(q, way).wait_send()
            own_copy(q, way).wait_send()
            sum_copy(q, way).wait_send()
        for out in out_copies(q):
            out.wait()

    for q in range(3):
        zred_copy(q).wait_send()


def on_device(values, exponents, expert_ids, route_weights, cotangent, w_gate, w_up, w_down):
    share = values.shape[1]
    d = lax.axis_index("dp")
    e = lax.axis_index("expert")
    odd = (d % 2) == 1
    blocks = exponents.shape[1]
    columns = d * share + jnp.arange(share, dtype=jnp.int32)
    block_map = ((columns // 128)[None, :] == jnp.arange(blocks, dtype=jnp.int32)[:, None]).astype(jnp.bfloat16)
    factor = jnp.dot(
        jnp.exp2(exponents.astype(jnp.float32)).astype(jnp.bfloat16), block_map,
        preferred_element_type=jnp.float32,
    )
    inputs = (values.astype(jnp.float32) * factor).astype(jnp.bfloat16)

    def placed(array):
        wide = jnp.zeros((TOK, BLK - share), jnp.bfloat16)
        return jnp.where(odd, jnp.concatenate([wide, array], 1), jnp.concatenate([array, wide], 1))

    mine = placed(jnp.where(odd, cotangent, inputs))
    give = placed(jnp.where(odd, inputs, cotangent))

    order = jnp.arange(16, dtype=jnp.int32)
    expert = order % 8 // 2 * 4 + order // 8 * 2 + order % 2
    hit = expert_ids.T[None, :, :] == expert[:, None, None]
    named = jnp.any(hit, axis=1)
    weight = jnp.sum(jnp.where(hit, route_weights.astype(jnp.float32).T[None], 0.0), axis=1)
    token = jnp.arange(TOK, dtype=jnp.int32)
    earlier = (token[:, None] < token[None, :]).astype(jnp.bfloat16)
    place = jnp.dot(named.astype(jnp.bfloat16), earlier, preferred_element_type=jnp.float32)
    chosen = named[:, None, :] & (
        place[:, None, :] == jnp.arange(SLOT, dtype=jnp.float32)[None, :, None]
    )
    pick = chosen.astype(jnp.bfloat16).reshape(16 * SLOT, TOK)
    pick_w = jnp.where(chosen, jnp.where(odd, weight, 1.0)[:, None, :], 0.0).astype(jnp.bfloat16)
    pick_w = pick_w.reshape(16 * SLOT, TOK)

    slab_row = jnp.arange(8 * SLOT, dtype=jnp.int32)
    dense_row = jnp.arange(HALF, dtype=jnp.int32)
    spread = (
        (slab_row[:, None] // SLOT == dense_row[None, :] // CAP)
        & (slab_row[:, None] % SLOT == dense_row[None, :] % CAP)
    ).astype(jnp.bfloat16)
    row_of = (jnp.arange(8, dtype=jnp.int32)[:, None] == dense_row[None, :] // CAP).astype(jnp.float32)
    slot_of = (dense_row[:, None] % CAP == jnp.arange(128, dtype=jnp.int32)[None, :]).astype(jnp.float32)

    vmem, hbm = pl.BlockSpec(memory_space=pltpu.VMEM), pl.BlockSpec(memory_space=pl.ANY)
    dma = pltpu.SemaphoreType.DMA
    bf, f32 = jnp.bfloat16, jnp.float32
    grad = jax.ShapeDtypeStruct((HID, FEAT), bf)
    res, back, gg, gu, gd = pl.pallas_call(
        kernel,
        out_shape=(
            jax.ShapeDtypeStruct((TOK, BLK), bf),
            jax.ShapeDtypeStruct((16, 16, 128), f32),
            grad, grad, grad,
        ),
        in_specs=[vmem] * 8 + [hbm] * 3,
        out_specs=(vmem, vmem, hbm, hbm, hbm),
        scratch_shapes=[
            pltpu.VMEM((TOK, BLK), bf),
            pltpu.VMEM((16, SLOT, BLK), bf),
            pltpu.VMEM((16, SLOT, BLK), bf),
            pltpu.VMEM((2, ROWS, FEAT), bf),
            pltpu.VMEM((2 * HPAD, FEAT), bf),
            pltpu.VMEM((HPAD, FEAT), bf),
            pltpu.VMEM((ROWS, 2 * HPAD), f32),
            pltpu.VMEM((ROWS, HPAD), f32),
            pltpu.VMEM((ROWS, 2 * HPAD), bf),
            pltpu.VMEM((ROWS, HPAD), bf),
            pltpu.VMEM((2 * HPAD, ROWS), bf),
            pltpu.VMEM((HPAD, ROWS), bf),
            pltpu.VMEM((ROWS, 128), f32),
            pltpu.VMEM((ROWS, FEAT), bf),
            pltpu.VMEM((4, 2, QTR, BLK), bf),
            pltpu.VMEM((4, 2, QTR, BLK), bf),
            pltpu.VMEM((4, 2, 2, QTR, BLK), bf),
            pltpu.VMEM((3, HALF, BLK), bf),
            pltpu.VMEM((3, HALF, BLK), bf),
            pltpu.VMEM((8, SLOT, BLK), bf),
            pltpu.VMEM((16, SLOT, BLK), bf),
            pltpu.VMEM((16, 128), f32),
            pltpu.VMEM((3, 16, 128), f32),
            pltpu.VMEM((4, 16, 128), f32),
            pltpu.VMEM((16, 128), f32),
            pltpu.VMEM((2 * HPAD, FEAT), bf),
            pltpu.VMEM((HPAD, FEAT), bf),
            dma((2,)), dma((16,)), dma((16,)), dma((3,)),
            dma((2, 4)), dma((2, 4)), dma((8, 2)), dma((8, 2)), dma((8, 2)), dma((8, 2)),
            dma((4, 2)), dma((4, 2)), dma((4, 2)), dma((4, 2)), dma((4, 2)), dma((4, 2)),
            dma((3,)), dma((3,)),
            dma((8,)), dma((16,)), dma((2,)), dma((6,)), dma((6,)), dma((16,)), dma((16,)),
            dma((4, 3)),
        ],
        compiler_params=pltpu.CompilerParams(
            collective_id=1, has_side_effects=True, vmem_limit_bytes=56 << 20
        ),
        name="moe_backward",
    )(mine, give, pick_w, pick, spread.T, spread, row_of, slot_of, w_gate[0], w_up[0], w_down[0])

    low = jnp.where(odd, res[:, share:], res[:, :share])
    d_values = (low.astype(f32) * factor).astype(bf)
    rank = e // 2 % 2 * 8 + e // 4 * 2 + e % 2
    own = lax.dynamic_index_in_dim(back, rank, 1, keepdims=False)
    per_expert = jnp.sum(jnp.where(chosen, own[:, :SLOT, None], 0.0), axis=1)
    per_route = jnp.sum(jnp.where(hit, per_expert[:, None, :], 0.0), axis=0).T
    d_route = (per_route / route_weights.astype(f32)).astype(bf)
    return d_values, d_route, gg[None], gu[None], gd[None]


def solution(mesh):
    in_specs = (
        P("expert", "dp"),
        P("expert", None),
        P("expert", None),
        P("expert", None),
        P("expert", "dp"),
        P("expert", "dp", None),
        P("expert", "dp", None),
        P("expert", "dp", None),
    )
    out_specs = (
        P("expert", "dp"),
        P("expert", None),
        P("expert", "dp", None),
        P("expert", "dp", None),
        P("expert", "dp", None),
    )
    return jax.shard_map(
        on_device, mesh=mesh, in_specs=in_specs, out_specs=out_specs, check_vma=False
    )
```

```python
import functools

import jax
import jax.numpy as jnp
from jax import lax
from jax.experimental import pallas as pl
from jax.experimental.pallas import tpu as pltpu
from jax.sharding import PartitionSpec as P

MESH = pl.DeviceIdType.MESH

SLOT = 48
CAP = 36
TOK = 128
BLK = 384
ZCOL = 2 * BLK
SHARE = 192
HID = 336
HPAD = 384
FEAT = 3072
ROWS = 16 * CAP
HALF = ROWS // 2
QTR = HALF // 2
PACK = 80
SIDE = 4 * PACK


def nt(left, right):
    return lax.dot_general(left, right, (((1,), (1,)), ((), ())), preferred_element_type=jnp.float32)


def tn(left, right):
    return lax.dot_general(left, right, (((0,), (0,)), ((), ())), preferred_element_type=jnp.float32)


def nn(left, right):
    return jnp.dot(left, right, preferred_element_type=jnp.float32)


def iota(shape, axis):
    return lax.broadcasted_iota(jnp.int32, shape, axis)


def over_cap(number):
    return (number * 1821) >> 16


def kernel(
    vt, ct, exps, ids, wts, wg, wu, wd,
    dv, droute, gg_out, gu_out, gd_out,
    inp, both, factor, pick, pick_t, pick_s, squeeze, spread, perm, row_of, slot_of, back, res, info, toks, sp,
    sendb, recvb, xs, ss, w2, w3, acc_gu, acc_h, hid, hidden, hid_t, hidden_t, prob, part,
    diag, dsum, ybuf, zsend, zrecv, retsend, retrecv, pbuf, py, pz, ptot, ogu, ogd,
    swap_sem, disp_send, disp_recv, w_sem, gz_send, gz_recv, gy_send, gy_recv, gd_send, gd_recv,
    info_send, info_recv, cy_send, cy_recv, ring_send, ring_recv, sib_send, sib_recv, sx_send, sx_recv,
    rd_send, rd_recv, ro_send, ro_recv, rs_send, rs_recv, rz_send, rz_recv,
    ret_send, ret_recv, fin_sem, p_send, p_recv, pb_send, pb_recv, out_sem,
):
    d = lax.axis_index("dp")
    e = lax.axis_index("expert")
    y, zl = lax.rem(d, 4), d // 4
    par, sub = lax.rem(y, 2), y // 2
    x, zh, c = e // 4, lax.rem(e // 2, 2), lax.rem(e, 2)
    rank = zh * 8 + c * 4 + x
    z8 = zh * 4 + zl

    def at_y(step):
        return (zl * 4 + lax.rem(y + step + 4, 4), e)

    def at_z(z):
        return (z * 4 + y, e)

    def at_ring(step):
        to = lax.rem(z8 + step + 8, 8)
        return (lax.rem(to, 4) * 4 + y, x * 4 + to // 4 * 2 + c)

    def expert_of(r):
        return lax.rem(r, 4) * 4 + r // 8 * 2 + lax.rem(r, 8) // 4

    def remote(src, dst, ssem, rsem, dev):
        return pltpu.make_async_remote_copy(src, dst, ssem, rsem, device_id=dev, device_id_type=MESH)

    bar = pltpu.get_barrier_semaphore()
    for step in (1, 2, 3):
        pl.semaphore_signal(bar, inc=1, device_id=at_y(step), device_id_type=MESH)
        pl.semaphore_signal(bar, inc=1, device_id=at_z(lax.rem(zl + step, 4)), device_id_type=MESH)
    for step in range(1, 16):
        pl.semaphore_signal(bar, inc=1, device_id=(d, lax.rem(e + step, 16)), device_id_type=MESH)

    for step in (1, 7):
        pl.semaphore_signal(bar, inc=1, device_id=at_ring(step), device_id_type=MESH)

    loads = [
        pltpu.make_async_copy(wg, w2.at[pl.ds(0, HID)], w_sem.at[0]),
        pltpu.make_async_copy(wu, w2.at[pl.ds(HPAD, HID)], w_sem.at[1]),
        pltpu.make_async_copy(wd, w3.at[pl.ds(0, HID)], w_sem.at[2]),
    ]
    for load in loads:
        load.start()

    block_of = (d * SHARE + iota((SHARE, 24), 0)) >> 7
    block_map = (block_of == iota((SHARE, 24), 1)).astype(jnp.bfloat16)
    factor[...] = nn(block_map, jnp.exp2(exps[...].astype(jnp.float32)).astype(jnp.bfloat16))
    inputs = (vt[...].astype(jnp.float32) * factor[...]).astype(jnp.bfloat16)

    order = iota((16, TOK), 0)
    expert = (order & 3) * 4 + (order >> 3) * 2 + ((order >> 2) & 1)
    wide = wts[...].astype(jnp.float32)
    named = jnp.zeros((16, TOK), jnp.float32)
    weight = jnp.zeros((16, TOK), jnp.float32)
    for k in range(4):
        hit = ids[pl.ds(k, 1), :] == expert
        named += jnp.where(hit, 1.0, 0.0)
        weight += jnp.where(hit, wide[k : k + 1, :], 0.0)
    earlier = jnp.where(iota((TOK, TOK), 0) < iota((TOK, TOK), 1), 1.0, 0.0).astype(jnp.bfloat16)
    place = nn(named.astype(jnp.bfloat16), earlier)
    place = jnp.where(named > 0.0, place, -1000.0)
    here = zh * 2 + c
    info[here, pl.ds(0, 16), :] = place
    info[here, pl.ds(16, 16), :] = weight

    partner = (zl * 4 + y + 1 - 2 * par, e)
    mine_at = pl.ds(pl.multiple_of(par * SHARE, 16), SHARE)
    other_at = pl.ds(pl.multiple_of((1 - par) * SHARE, 16), SHARE)
    inp[...] = inputs
    both[mine_at, :] = inputs
    own_lanes = pl.ds(pl.multiple_of(c * TOK, 128), TOK)
    toks[zh, pl.ds(pl.multiple_of(d * SHARE, 16), SHARE), own_lanes] = ct[...]

    def cot_copy(j):
        ref = toks.at[zh, pl.ds(pl.multiple_of(d * SHARE, 16), SHARE), own_lanes]
        return remote(ref, ref, cy_send.at[j - 1], cy_recv.at[j - 1], at_y(j))

    def info_copy(j):
        to = x * 4 + lax.rem(zh + j // 2, 2) * 2 + lax.rem(c + j, 2)
        return remote(info.at[here], info.at[here], info_send.at[j - 1], info_recv.at[j - 1], (d, to))

    pl.semaphore_wait(bar, 23)
    for j in (1, 2, 3):
        cot_copy(j).start()
    for j in (1, 2, 3):
        info_copy(j).start()
    swap = remote(inp, both.at[mine_at], swap_sem.at[0], swap_sem.at[1], partner)
    swap.start()

    slots = iota((SLOT, TOK), 0).astype(jnp.float32)
    for r in range(16):
        chosen = place[r : r + 1, :] == slots
        pick[pl.ds(r * SLOT, SLOT), :] = jnp.where(chosen, 1.0, 0.0).astype(jnp.bfloat16)
    dense = iota((QTR, 4 * SLOT), 0)
    squeeze[...] = jnp.where(
        iota((QTR, 4 * SLOT), 1) == dense + over_cap(dense) * (SLOT - CAP), 1.0, 0.0
    ).astype(jnp.bfloat16)

    def tok_block(o, half=None):
        src = lax.rem(z8 - o + 8, 8)
        low, count = (0, ZCOL) if half is None else (half * BLK, BLK)
        return toks.at[src // 4, pl.ds(pl.multiple_of(lax.rem(src, 4) * ZCOL + low, 16), count), own_lanes]

    def ring_copy(k, way):
        o = k - 1 if way == 0 else lax.rem(9 - k, 8)
        if k == 4:
            ref = tok_block(o, way)
        else:
            ref = tok_block(o)
        return remote(ref, ref, ring_send.at[way, k - 1], ring_recv.at[way, k - 1], at_ring(1 if way == 0 else 7))

    def ring_arrival(k, way):
        o = k if way == 0 else 8 - k
        if k == 4:
            ref = tok_block(o, way)
        else:
            ref = tok_block(o)
        return remote(ref, ref, ring_send.at[way, k - 1], ring_recv.at[way, k - 1], at_ring(1 if way == 0 else 7))

    def sib_copy(o):
        ref = tok_block(o)
        return remote(ref, ref, sib_send.at[o], sib_recv.at[o], (d, e + 1 - 2 * c))

    for j in (1, 2, 3):
        cot_copy(j).wait_recv()
    for way in (0, 1):
        ring_copy(1, way).start()
    sib_copy(0).start()

    swap.wait()

    @pl.when(c == par)
    def _():
        picked = nt(pick[...], both[...]).astype(jnp.bfloat16)
        for r in range(16):
            sendb[r] = picked[r * SLOT : (r + 1) * SLOT]

    def slot_at(r):
        return r // 8 * 4 + lax.rem(r, 4)

    def dispatch(r):
        return remote(sendb.at[r], recvb.at[slot_at(rank)], disp_send.at[r], disp_recv.at[rank], (d, expert_of(r)))

    def arrival(r):
        return remote(sendb.at[rank], recvb.at[slot_at(r)], disp_send.at[rank], disp_recv.at[r], (d, expert_of(r)))

    @pl.when(c == par)
    def _():
        @pl.loop(0, 16)
        def _(i):
            r = lax.rem(i + zh * 8, 16)

            @pl.when(r != rank)
            def _():
                dispatch(r).start()

        recvb[slot_at(rank)] = sendb[rank]

    for j in (1, 2, 3):
        info_copy(j).wait_recv()
    packed = iota((PACK, TOK), 0).astype(jnp.float32)
    for b in range(4):
        for to in range(4):
            row = zh * 8 + c * 4 + to
            chosen = info[b, pl.ds(row, 1), :] + float(CAP * (b % 2)) == packed
            pick_s[b // 2, pl.ds(to * PACK, PACK), pl.ds(b % 2 * TOK, TOK)] = jnp.where(
                chosen, info[b, pl.ds(row + 16, 1), :], 0.0
            ).astype(jnp.bfloat16)

    def s_rows(src, who, count):
        return pl.ds(pl.multiple_of(src // 4 * SIDE + who * PACK, 16), count)

    def s_cols(src):
        return pl.ds(pl.multiple_of(lax.rem(src, 4) * ZCOL, 128), ZCOL)

    def sx_copy(o, j):
        src = lax.rem(z8 - o + 8, 8)
        to = lax.rem(x + j, 4)
        return remote(sp.at[s_rows(src, to, PACK), s_cols(src)], ss.at[s_rows(src, x, PACK), s_cols(src)],
                      sx_send.at[o, j - 1], sx_recv.at[o, j - 1], (d, to * 4 + zh * 2 + c))

    def pick_chunk(o):
        sib_copy(o).wait_recv()
        src = lax.rem(z8 - o + 8, 8)
        sp[s_rows(src, 0, SIDE), s_cols(src)] = nt(pick_s[src // 4], toks[src // 4, s_cols(src), :]).astype(jnp.bfloat16)
        for j in (1, 3, 2):
            sx_copy(o, j).start()
        ss[s_rows(src, x, PACK), s_cols(src)] = sp[s_rows(src, x, PACK), s_cols(src)]

    def ring_step(k):
        for way in (0, 1):
            ring_arrival(k, way).wait_recv()
            if k < 4:
                ring_copy(k + 1, way).start()
        if k < 4:
            sib_copy(k).start()
            sib_copy(8 - k).start()
            pick_chunk(k)
            pick_chunk(8 - k)
        else:
            sib_copy(4).start()
            pick_chunk(4)

    def s_chunk(m):
        o = jnp.where(lax.rem(m, 2) == 1, (m + 1) // 2, lax.rem(8 - m // 2, 8))
        src = lax.rem(z8 - o + 8, 8)
        for j in (1, 2, 3):
            sx_copy(o, j).wait_recv()
        rows = s_rows(src, 0, SIDE)
        acc_h[rows, :] += nt(ss[rows, s_cols(src)], w3[:, s_cols(src)])

    pick_chunk(0)
    dense = iota((4 * SLOT, QTR), 1)
    spread[...] = jnp.where(
        iota((4 * SLOT, QTR), 0) == dense + over_cap(dense) * (SLOT - CAP), 1.0, 0.0
    ).astype(jnp.bfloat16)
    dense = iota((HALF, SIDE), 0)
    which = over_cap(dense)
    perm[...] = jnp.where(
        iota((HALF, SIDE), 1) == (which & 3) * PACK + (which >> 2) * CAP + dense - which * CAP, 1.0, 0.0
    ).astype(jnp.bfloat16)
    row_of[...] = jnp.where(over_cap(iota((8, HALF), 1)) == iota((8, HALF), 0), 1.0, 0.0)
    dense = iota((HALF, 128), 0)
    slot_of[...] = jnp.where(dense - over_cap(dense) * CAP == iota((HALF, 128), 1), 1.0, 0.0)
    for h in (0, 1):
        pick_t[h] = pick[pl.ds(h * 8 * SLOT, 8 * SLOT), :].T
    w2[pl.ds(HID, HPAD - HID), :] = jnp.zeros((HPAD - HID, FEAT), jnp.bfloat16)
    w2[pl.ds(HPAD + HID, HPAD - HID), :] = jnp.zeros((HPAD - HID, FEAT), jnp.bfloat16)
    w3[pl.ds(HID, HPAD - HID), :] = jnp.zeros((HPAD - HID, FEAT), jnp.bfloat16)
    acc_gu[...] = jnp.zeros_like(acc_gu)
    acc_h[...] = jnp.zeros_like(acc_h)

    def block(h, z, yy, lo=0, rows=QTR):
        return xs.at[pl.ds(pl.multiple_of(h * HALF + lax.rem(yy, 2) * QTR + lo, 16), rows),
                     pl.ds(pl.multiple_of(z * ZCOL + yy // 2 * BLK, 128), BLK)]

    def z_copy(h, z, way):
        ref = block(h, z, y)
        return remote(ref, ref, gz_send.at[h * 4 + z, way], gz_recv.at[h * 4 + z], at_z(zl + 1 - 2 * way))

    def z_arrival(h, z):
        ref = block(h, z, y)
        return remote(ref, ref, gz_send.at[h * 4 + z, 0], gz_recv.at[h * 4 + z], at_z(lax.rem(zl + 1, 4)))

    def z_each(h, z, what):
        @pl.when(jnp.logical_and(z <= zl, zl < 3))
        def _():
            what(z_copy(h, z, 0))

        @pl.when(jnp.logical_and(z >= zl, zl > 0))
        def _():
            what(z_copy(h, z, 1))

    def take_half(h):
        @pl.loop(0, 4)
        def _(k):
            r = h * 8 + par * 4 + k

            @pl.when(r != rank)
            def _():
                arrival(r).wait_recv()

        slabs = recvb[pl.ds(h * 4, 4)].reshape(4 * SLOT, BLK)
        xs[pl.ds(pl.multiple_of(h * HALF + par * QTR, 16), QTR),
           pl.ds(pl.multiple_of(zl * ZCOL + sub * BLK, 128), BLK)] = nn(squeeze[...], slabs).astype(jnp.bfloat16)
        z_each(h, zl, lambda copy: copy.start())

    def chunk(s):
        i, j = s // 4, lax.rem(s, 4)
        h = lax.rem(zh + i, 2)
        first, second, third = zl + 1 - 2 * (zl // 2), lax.rem(2 + 3 * zl, 5), 3 - 3 * (zl // 2)
        z = jnp.where(j == 0, zl, jnp.where(j == 1, first, jnp.where(j == 2, second, third)))
        return h, j, z

    left, right = lax.rem(y + 3, 4), lax.rem(y + 1, 4)
    across = lax.rem(y + 2, 4)

    def y_copy(s, way):
        h, j, z = chunk(s)
        ref = block(h, z, y)
        return remote(ref, ref, gy_send.at[s, way], gy_recv.at[s, way], at_y(1 if way == 0 else 3))

    def y_arrival(s, way):
        h, j, z = chunk(s)
        ref = block(h, z, left if way == 0 else right)
        return remote(ref, ref, gy_send.at[s, way], gy_recv.at[s, way], at_y(1 if way == 0 else 3))

    CUT = ((0, 80), (80, 64))

    def turn(n, way):
        return 1 + 2 * lax.rem(n + way, 2)

    def d_copy(s, way):
        h, j, z = chunk(s)
        ref = block(h, z, lax.rem(y + 4 - turn(s, way), 4), *CUT[way])
        return remote(ref, ref, gd_send.at[s, way], gd_recv.at[s, way], at_y(turn(s, way)))

    def d_arrival(s, way):
        h, j, z = chunk(s)
        ref = block(h, z, across, *CUT[way])
        return remote(ref, ref, gd_send.at[s, way], gd_recv.at[s, way], at_y(turn(s, way)))

    take_half(zh)
    y_copy(0, 0).start()
    y_copy(0, 1).start()
    for load in loads:
        load.wait()

    @pl.loop(0, 9)
    def _(s):
        @pl.when(s == 3)
        def _():
            take_half(1 - zh)

        @pl.when(s < 7)
        def _():
            h, j, z = chunk(s + 1)

            @pl.when(j > 0)
            def _():
                z_arrival(h, z).wait_recv()
                z_each(h, z, lambda copy: copy.start())

            y_copy(s + 1, 0).start()
            y_copy(s + 1, 1).start()

        @pl.when(s < 8)
        def _():
            for way in (0, 1):
                y_arrival(s, way).wait_recv()
            for way in (0, 1):
                d_copy(s, way).start()

        for k in (1, 2, 3, 4):
            @pl.when(s == k)
            def _(k=k):
                ring_step(k)

        @pl.when(s > 0)
        def _():
            for way in (0, 1):
                d_arrival(s - 1, way).wait_recv()
            h, j, z = chunk(s - 1)
            rows = pl.ds(pl.multiple_of(h * HALF, 16), HALF)
            cols = pl.ds(pl.multiple_of(z * ZCOL, 128), ZCOL)
            acc_gu[rows, :] += nt(xs[rows, cols], w2[:, cols])

            @pl.when(j == 3)
            def _():
                @pl.loop(0, HALF // 32)
                def _(b):
                    part_rows = pl.ds(pl.multiple_of(h * HALF + b * 32, 16), 32)
                    gate = acc_gu[part_rows, pl.ds(0, HPAD)]
                    upper = acc_gu[part_rows, pl.ds(HPAD, HPAD)]
                    sig = jax.nn.sigmoid(gate)
                    swished = gate * sig
                    hidden[part_rows, :] = (swished * upper).astype(jnp.bfloat16)
                    acc_gu[part_rows, pl.ds(0, HPAD)] = upper * sig * (1.0 + gate * (1.0 - sig))
                    acc_gu[part_rows, pl.ds(HPAD, HPAD)] = swished

        @pl.when(s > 2)
        def _():
            s_chunk(s - 3)

    for h in (0, 1):
        hidden_t[:, pl.ds(h * SIDE, SIDE)] = nn(hidden[pl.ds(h * HALF, HALF), :].T, perm[...]).astype(jnp.bfloat16)
    s_chunk(6)
    s_chunk(7)

    for h in (0, 1):
        grad = acc_h[pl.ds(h * SIDE, SIDE), :]
        high = grad.astype(jnp.bfloat16)
        low = (grad - high.astype(jnp.float32)).astype(jnp.bfloat16)
        acc_h[pl.ds(h * HALF, HALF), :] = nn(perm[...], high) + nn(perm[...], low)

    @pl.loop(0, ROWS // 32)
    def _(b):
        part_rows = pl.ds(pl.multiple_of(b * 32, 16), 32)
        grad = acc_h[part_rows, :]
        hid[part_rows, pl.ds(0, HPAD)] = (grad * acc_gu[part_rows, pl.ds(0, HPAD)]).astype(jnp.bfloat16)
        hid[part_rows, pl.ds(HPAD, HPAD)] = (grad * acc_gu[part_rows, pl.ds(HPAD, HPAD)]).astype(jnp.bfloat16)
        total = jnp.sum(hidden[part_rows, :].astype(jnp.float32) * grad, axis=1, keepdims=True)
        prob[part_rows, :] = jnp.broadcast_to(total, (32, 128))

    for h in (0, 1):
        pbuf[pl.ds(h * 8, 8), :] = jnp.dot(
            row_of[...], prob[pl.ds(h * HALF, HALF), :] * slot_of[...],
            precision=lax.Precision.HIGHEST, preferred_element_type=jnp.float32,
        )

    def p_y(j):
        return remote(pbuf, py.at[j - 1], p_send.at[j - 1], p_recv.at[j - 1], at_y(j))

    def p_z(j):
        return remote(pz.at[3], pz.at[j - 1], p_send.at[2 + j], p_recv.at[2 + j], at_z(lax.rem(zl + j, 4)))

    def p_b(step):
        return remote(ptot, back.at[rank], pb_send.at[step], pb_recv.at[rank],
                      (d, lax.rem(e + step, 16)))

    for j in (1, 2, 3):
        p_y(j).start()

    def rs_step(n):
        i, q = n // 4, lax.rem(n, 4)
        return lax.rem(zh + 1 + i, 2), lax.rem(zl + 1 + q, 4)

    def piece(yy, n, lo, rows):
        h, z = rs_step(n)
        return (pl.ds(pl.multiple_of(h * HALF + lax.rem(yy, 2) * QTR + lo, 16), rows),
                pl.ds(pl.multiple_of(z * ZCOL + yy // 2 * BLK, 128), BLK))

    def diag_copy(n, way):
        lo, rows = CUT[way]
        return remote(part.at[piece(across, n, lo, rows)], diag.at[n, pl.ds(lo, rows)],
                      rd_send.at[n, way], rd_recv.at[n, way], at_y(turn(n, way)))

    def own_copy(n, way):
        lo, rows = CUT[1 - way]
        to = lax.rem(y + turn(n, way), 4)
        return remote(part.at[piece(to, n, lo, rows)], ybuf.at[n, way, pl.ds(lo, rows)],
                      ro_send.at[n, way], ro_recv.at[n, way], at_y(turn(n, way)))

    def sum_copy(n, way):
        lo, rows = CUT[way]
        return remote(dsum.at[n, pl.ds(lo, rows)], ybuf.at[n, way, pl.ds(lo, rows)],
                      rs_send.at[n, way], rs_recv.at[n, way], at_y(turn(n, way)))

    def zred_copy(n):
        return remote(zsend.at[n], zrecv.at[n], rz_send.at[n], rz_recv.at[n], at_z(rs_step(n)[1]))

    def make_part(n):
        h, z = rs_step(n)
        rows = pl.ds(pl.multiple_of(h * HALF, 16), HALF)
        cols = pl.ds(pl.multiple_of(z * ZCOL, 128), ZCOL)
        part[rows, cols] = nn(hid[rows, :], w2[:, cols]).astype(jnp.bfloat16)
        for way in (0, 1):
            diag_copy(n, way).start()
        for way in (0, 1):
            own_copy(n, way).start()

    def out_copies(q):
        cols = pl.ds(pl.multiple_of(q * ZCOL, 128), ZCOL)
        return (
            pltpu.make_async_copy(ogu.at[pl.ds(0, HID), cols], gg_out.at[:, cols], out_sem.at[q, 0]),
            pltpu.make_async_copy(ogu.at[pl.ds(HPAD, HID), cols], gu_out.at[:, cols], out_sem.at[q, 1]),
            pltpu.make_async_copy(ogd.at[pl.ds(0, HID), cols], gd_out.at[:, cols], out_sem.at[q, 2]),
        )

    def weight_grads(q):
        cols = pl.ds(pl.multiple_of(q * ZCOL, 128), ZCOL)
        ogu[:, cols] = nn(hid_t[...], xs[:, cols]).astype(jnp.bfloat16)
        ogd[:, cols] = nn(hidden_t[...], ss[:, cols]).astype(jnp.bfloat16)
        for out in out_copies(q):
            out.start()

    def y_sum(n):
        for way in (0, 1):
            own_copy(n, way).wait_recv()
            sum_copy(n, way).wait_recv()
        own = part[piece(y, n, 0, QTR)].astype(jnp.float32)
        return own + (ybuf[n, 0].astype(jnp.float32) + ybuf[n, 1].astype(jnp.float32))

    def ret_rank(i, k):
        return lax.rem(zh + 1 + i, 2) * 8 + par * 4 + k

    def ret_copy(i, k):
        return remote(retsend.at[i * 4 + k], retrecv.at[rank], ret_send.at[i * 4 + k], ret_recv.at[rank],
                      (d, expert_of(ret_rank(i, k))))

    def ret_arrival(r):
        return remote(retsend.at[0], retrecv.at[r], ret_send.at[0], ret_recv.at[r], (d, expert_of(r)))

    def send_back(i):
        total = y_sum(i * 4 + 3)
        for q in range(3):
            zred_copy(i * 4 + q).wait_recv()
            total += zrecv[i * 4 + q].astype(jnp.float32)
        slabs = nn(spread[...], total.astype(jnp.bfloat16)).astype(jnp.bfloat16)
        for k in range(4):
            retsend[i * 4 + k] = slabs[k * SLOT : (k + 1) * SLOT]
            if i == 0:
                ret_copy(i, k).start()
            else:
                @pl.when(ret_rank(i, k) != rank)
                def _(k=k):
                    ret_copy(i, k).start()

                @pl.when(ret_rank(i, k) == rank)
                def _(k=k):
                    retrecv[rank] = slabs[k * SLOT : (k + 1) * SLOT]

    make_part(0)
    hid_t[...] = hid[...].T

    @pl.loop(0, 8)
    def _(n):
        @pl.when(n < 7)
        def _():
            make_part(n + 1)

        for way in (0, 1):
            diag_copy(n, way).wait_recv()
            lo, rows = CUT[way]
            to = lax.rem(y + turn(n, way), 4)
            dsum[n, pl.ds(lo, rows)] = (
                part[piece(to, n, lo, rows)].astype(jnp.float32)
                + diag[n, pl.ds(lo, rows)].astype(jnp.float32)
            ).astype(jnp.bfloat16)
            sum_copy(n, way).start()

        @pl.when(n < 4)
        def _():
            weight_grads(n)

        @pl.when(n == 1)
        def _():
            for j in (1, 2, 3):
                p_y(j).wait_recv()
            pz[3] = pbuf[...] + py[0] + py[1] + py[2]
            for j in (1, 2, 3):
                p_z(j).start()

        @pl.when(n == 3)
        def _():
            for j in (1, 2, 3):
                p_z(j).wait_recv()
            ptot[...] = pz[0] + pz[1] + pz[2] + pz[3]
            back[rank] = ptot[...]

            @pl.loop(1, 16)
            def _(step):
                p_b(step).start()

        @pl.when(jnp.logical_and(n > 0, n != 4))
        def _():
            zsend[n - 1] = y_sum(n - 1).astype(jnp.bfloat16)
            zred_copy(n - 1).start()

        @pl.when(n == 4)
        def _():
            send_back(0)

    send_back(1)

    @pl.loop(0, 16)
    def _(r):
        @pl.when(r != rank)
        def _():
            remote(ptot, back.at[r], pb_send.at[0], pb_recv.at[r], (d, expert_of(r))).wait_recv()

    own = jnp.concatenate([back[r, pl.ds(rank, 1), :] for r in range(16)], axis=0)
    own_t = jnp.concatenate([own, jnp.zeros((112, 128), jnp.float32)], axis=0).T
    per_expert = jnp.concatenate(
        [
            jnp.sum(pick[pl.ds(r * SLOT, SLOT), :].astype(jnp.float32) * own_t[:SLOT, r : r + 1],
                    axis=0, keepdims=True)
            for r in range(16)
        ],
        axis=0,
    )
    grads = [
        jnp.sum(jnp.where(ids[pl.ds(k, 1), :] == expert, per_expert, 0.0), axis=0, keepdims=True)
        for k in range(4)
    ]
    droute[...] = (jnp.concatenate(grads, axis=0) / wts[...].astype(jnp.float32)).astype(jnp.bfloat16)

    fin = remote(res.at[other_at], res.at[other_at], fin_sem.at[0], fin_sem.at[1], partner)

    @pl.when(c == par)
    def _():
        def from_half(h):
            @pl.loop(0, 8)
            def _(k):
                @pl.when(h * 8 + k != rank)
                def _():
                    ret_arrival(h * 8 + k).wait_recv()

            return nn(pick_t[h], retrecv[pl.ds(h * 8, 8)].reshape(8 * SLOT, BLK))

        total = from_half(1 - zh)
        total += from_half(zh)
        res[...] = total.T.astype(jnp.bfloat16)
        fin.start()
        fin.wait_send()

    @pl.when(c != par)
    def _():
        fin.wait_recv()

    dv[...] = (res[mine_at, :].astype(jnp.float32) * factor[...]).astype(jnp.bfloat16)

    @pl.loop(0, 16)
    def _(r):
        @pl.when(jnp.logical_and(r != rank, c == par))
        def _():
            dispatch(r).wait_send()

    for j in (1, 2, 3):
        cot_copy(j).wait_send()
        info_copy(j).wait_send()
    for k in (1, 2, 3, 4):
        for way in (0, 1):
            ring_copy(k, way).wait_send()

    @pl.loop(0, 8)
    def _(o):
        sib_copy(o).wait_send()
        for j in (1, 2, 3):
            sx_copy(o, j).wait_send()

    @pl.loop(1, 16)
    def _(step):
        p_b(step).wait_send()

    for k in range(4):
        ret_copy(0, k).wait_send()

        @pl.when(ret_rank(1, k) != rank)
        def _(k=k):
            ret_copy(1, k).wait_send()

    @pl.loop(0, 8)
    def _(s):
        for way in (0, 1):
            y_copy(s, way).wait_send()
            d_copy(s, way).wait_send()
            diag_copy(s, way).wait_send()
            own_copy(s, way).wait_send()
            sum_copy(s, way).wait_send()

    @pl.loop(0, 8)
    def _(s):
        z_each(s // 4, lax.rem(s, 4), lambda copy: copy.wait_send())

    for j in (1, 2, 3):
        p_y(j).wait_send()
        p_z(j).wait_send()

    @pl.loop(0, 4)
    def _(q):
        for out in out_copies(q):
            out.wait()

    for q in range(3):
        zred_copy(q).wait_send()
        zred_copy(4 + q).wait_send()


def finish(dv_in, droute_in, gg_in, gu_in, gd_in, dv, droute, gg, gu, gd, small, tiny, held, in_sem, out_sem):
    trips = [(dv_in, small, dv), (droute_in, tiny, droute)]
    for part in range(3):
        cols = pl.ds(part * 1024, 1024)
        for i, (src, dst) in enumerate(((gg_in, gg), (gu_in, gu), (gd_in, gd))):
            trips.append((src.at[:, cols], held.at[i, :, cols], dst.at[:, cols]))
    loads = [pltpu.make_async_copy(src, mid, in_sem.at[i]) for i, (src, mid, _) in enumerate(trips)]
    stores = [pltpu.make_async_copy(mid, dst, out_sem.at[i]) for i, (_, mid, dst) in enumerate(trips)]
    for load in loads:
        load.start()
    for load, store in zip(loads, stores):
        load.wait()
        store.start()
    for store in stores:
        store.wait()


def on_device(values, exponents, expert_ids, route_weights, cotangent, w_gate, w_up, w_down):
    vmem, hbm = pl.BlockSpec(memory_space=pltpu.VMEM), pl.BlockSpec(memory_space=pl.ANY)
    dma = pltpu.SemaphoreType.DMA
    bf, f32 = jnp.bfloat16, jnp.float32
    grad = jax.ShapeDtypeStruct((HID, FEAT), bf)
    outs = pl.pallas_call(
        kernel,
        out_shape=(
            jax.ShapeDtypeStruct((SHARE, TOK), bf),
            jax.ShapeDtypeStruct((4, TOK), bf),
            grad, grad, grad,
        ),
        in_specs=[vmem] * 5 + [hbm] * 3,
        out_specs=(vmem, vmem, hbm, hbm, hbm),
        scratch_shapes=[
            pltpu.VMEM((SHARE, TOK), bf),
            pltpu.VMEM((BLK, TOK), bf),
            pltpu.VMEM((SHARE, TOK), f32),
            pltpu.VMEM((16 * SLOT, TOK), bf),
            pltpu.VMEM((2, TOK, 8 * SLOT), bf),
            pltpu.VMEM((2, SIDE, 2 * TOK), bf),
            pltpu.VMEM((QTR, 4 * SLOT), bf),
            pltpu.VMEM((4 * SLOT, QTR), bf),
            pltpu.VMEM((HALF, SIDE), bf),
            pltpu.VMEM((8, HALF), f32),
            pltpu.VMEM((HALF, 128), f32),
            pltpu.VMEM((16, 16, 128), f32),
            pltpu.VMEM((BLK, TOK), bf),
            pltpu.VMEM((4, 32, TOK), f32),
            pltpu.VMEM((2, FEAT, 2 * TOK), bf),
            pltpu.VMEM((2 * SIDE, FEAT), bf),
            pltpu.VMEM((16, SLOT, BLK), bf),
            pltpu.VMEM((8, SLOT, BLK), bf),
            pltpu.VMEM((ROWS, FEAT), bf),
            pltpu.VMEM((2 * SIDE, FEAT), bf),
            pltpu.VMEM((2 * HPAD, FEAT), bf),
            pltpu.VMEM((HPAD, FEAT), bf),
            pltpu.VMEM((ROWS, 2 * HPAD), f32),
            pltpu.VMEM((2 * SIDE, HPAD), f32),
            pltpu.VMEM((ROWS, 2 * HPAD), bf),
            pltpu.VMEM((ROWS, HPAD), bf),
            pltpu.VMEM((2 * HPAD, ROWS), bf),
            pltpu.VMEM((HPAD, 2 * SIDE), bf),
            pltpu.VMEM((ROWS, 128), f32),
            pltpu.VMEM((ROWS, FEAT), bf),
            pltpu.VMEM((8, QTR, BLK), bf),
            pltpu.VMEM((8, QTR, BLK), bf),
            pltpu.VMEM((8, 2, QTR, BLK), bf),
            pltpu.VMEM((8, QTR, BLK), bf),
            pltpu.VMEM((8, QTR, BLK), bf),
            pltpu.VMEM((8, SLOT, BLK), bf),
            pltpu.VMEM((16, SLOT, BLK), bf),
            pltpu.VMEM((16, 128), f32),
            pltpu.VMEM((3, 16, 128), f32),
            pltpu.VMEM((4, 16, 128), f32),
            pltpu.VMEM((16, 128), f32),
            pltpu.VMEM((2 * HPAD, FEAT), bf),
            pltpu.VMEM((HPAD, FEAT), bf),
            dma((2,)), dma((16,)), dma((16,)), dma((3,)),
            dma((8, 2)), dma((8,)), dma((8, 2)), dma((8, 2)), dma((8, 2)), dma((8, 2)),
            dma((3,)), dma((3,)), dma((3,)), dma((3,)), dma((2, 4)), dma((2, 4)), dma((8,)), dma((8,)),
            dma((8, 3)), dma((8, 3)),
            dma((8, 2)), dma((8, 2)), dma((8, 2)), dma((8, 2)), dma((8, 2)), dma((8, 2)),
            dma((8,)), dma((8,)),
            dma((8,)), dma((16,)), dma((2,)), dma((6,)), dma((6,)), dma((16,)), dma((16,)),
            dma((4, 3)),
        ],
        compiler_params=pltpu.CompilerParams(
            collective_id=1, has_side_effects=True, vmem_limit_bytes=56 << 20
        ),
        name="moe_backward",
    )(values.T, cotangent.T, exponents.T, expert_ids.T, route_weights.T, w_gate[0], w_up[0], w_down[0])
    dv, droute, gg, gu, gd = pl.pallas_call(
        finish,
        out_shape=[jax.ShapeDtypeStruct(out.shape, bf) for out in outs],
        in_specs=[hbm] * 5,
        out_specs=[hbm] * 5,
        scratch_shapes=[
            pltpu.VMEM((SHARE, TOK), bf),
            pltpu.VMEM((4, TOK), bf),
            pltpu.VMEM((3, HID, FEAT), bf),
            dma((11,)), dma((11,)),
        ],
        cost_estimate=pl.CostEstimate(flops=0, bytes_accessed=12 << 20, transcendentals=0),
        name="finish",
    )(*outs)
    return dv.T, droute.T, gg[None], gu[None], gd[None]


def solution(mesh):
    in_specs = (
        P("expert", "dp"),
        P("expert", None),
        P("expert", None),
        P("expert", None),
        P("expert", "dp"),
        P("expert", "dp", None),
        P("expert", "dp", None),
        P("expert", "dp", None),
    )
    out_specs = (
        P("expert", "dp"),
        P("expert", None),
        P("expert", "dp", None),
        P("expert", "dp", None),
        P("expert", "dp", None),
    )
    return jax.shard_map(
        on_device, mesh=mesh, in_specs=in_specs, out_specs=out_specs, check_vma=False
    )
```

```python
import functools

import jax
import jax.numpy as jnp
from jax import lax
from jax.experimental import pallas as pl
from jax.experimental.pallas import tpu as pltpu
from jax.sharding import PartitionSpec as P

MESH = pl.DeviceIdType.MESH

SLOT = 48
CAP = 36
TOK = 128
BLK = 384
ZCOL = 2 * BLK
SHARE = 192
HID = 336
HPAD = 384
FEAT = 3072
ROWS = 16 * CAP
HALF = ROWS // 2
QTR = HALF // 2
PACK = 80
SIDE = 4 * PACK


def nt(left, right):
    return lax.dot_general(left, right, (((1,), (1,)), ((), ())), preferred_element_type=jnp.float32)


def tn(left, right):
    return lax.dot_general(left, right, (((0,), (0,)), ((), ())), preferred_element_type=jnp.float32)


def nn(left, right):
    return jnp.dot(left, right, preferred_element_type=jnp.float32)


def iota(shape, axis):
    return lax.broadcasted_iota(jnp.int32, shape, axis)


def over_cap(number):
    return (number * 1821) >> 16


def kernel(
    vt, ct, exps, ids, wts, wg, wu, wd,
    dv, droute, gg_out, gu_out, gd_out,
    inp, both, factor, pick, pick_t, pick_s, squeeze, spread, perm, row_of, slot_of, back, res, info, toks, sp,
    sendb, recvb, xs, ss, w2, w3, acc_gu, acc_h, grad_x, hid, hidden, hid_t, hidden_t, prob, part,
    diag, dsum, ybuf, zsend, zrecv, retsend, retrecv, pbuf, py, pz, ptot, ogu, ogd,
    swap_sem, disp_send, disp_recv, w_sem, gz_send, gz_recv, gy_send, gy_recv, gd_send, gd_recv,
    info_send, info_recv, cy_send, cy_recv, ring_send, ring_recv, sib_send, sib_recv, sx_send, sx_recv,
    rd_send, rd_recv, ro_send, ro_recv, rs_send, rs_recv, rz_send, rz_recv,
    ret_send, ret_recv, fin_sem, p_send, p_recv, pb_send, pb_recv, out_sem,
):
    d = lax.axis_index("dp")
    e = lax.axis_index("expert")
    y, zl = lax.rem(d, 4), d // 4
    par, sub = lax.rem(y, 2), y // 2
    x, zh, c = e // 4, lax.rem(e // 2, 2), lax.rem(e, 2)
    rank = zh * 8 + c * 4 + x
    z8 = zh * 4 + zl

    def at_y(step):
        return (zl * 4 + lax.rem(y + step + 4, 4), e)

    def at_z(z):
        return (z * 4 + y, e)

    def at_ring(step):
        to = lax.rem(z8 + step + 8, 8)
        return (lax.rem(to, 4) * 4 + y, x * 4 + to // 4 * 2 + c)

    def expert_of(r):
        return lax.rem(r, 4) * 4 + r // 8 * 2 + lax.rem(r, 8) // 4

    def remote(src, dst, ssem, rsem, dev):
        return pltpu.make_async_remote_copy(src, dst, ssem, rsem, device_id=dev, device_id_type=MESH)

    bar = pltpu.get_barrier_semaphore()
    for step in (1, 2, 3):
        pl.semaphore_signal(bar, inc=1, device_id=at_y(step), device_id_type=MESH)
        pl.semaphore_signal(bar, inc=1, device_id=at_z(lax.rem(zl + step, 4)), device_id_type=MESH)
    for step in range(1, 16):
        pl.semaphore_signal(bar, inc=1, device_id=(d, lax.rem(e + step, 16)), device_id_type=MESH)

    for step in (1, 7):
        pl.semaphore_signal(bar, inc=1, device_id=at_ring(step), device_id_type=MESH)

    loads = [
        pltpu.make_async_copy(wg, w2.at[pl.ds(0, HID)], w_sem.at[0]),
        pltpu.make_async_copy(wu, w2.at[pl.ds(HPAD, HID)], w_sem.at[1]),
        pltpu.make_async_copy(wd, w3.at[pl.ds(0, HID)], w_sem.at[2]),
    ]
    for load in loads:
        load.start()

    block_of = (d * SHARE + iota((SHARE, 24), 0)) >> 7
    block_map = (block_of == iota((SHARE, 24), 1)).astype(jnp.bfloat16)
    factor[...] = nn(block_map, jnp.exp2(exps[...].astype(jnp.float32)).astype(jnp.bfloat16))
    inputs = (vt[...].astype(jnp.float32) * factor[...]).astype(jnp.bfloat16)

    order = iota((16, TOK), 0)
    expert = (order & 3) * 4 + (order >> 3) * 2 + ((order >> 2) & 1)
    wide = wts[...].astype(jnp.float32)
    named = jnp.zeros((16, TOK), jnp.float32)
    weight = jnp.zeros((16, TOK), jnp.float32)
    for k in range(4):
        hit = ids[pl.ds(k, 1), :] == expert
        named += jnp.where(hit, 1.0, 0.0)
        weight += jnp.where(hit, wide[k : k + 1, :], 0.0)
    earlier = jnp.where(iota((TOK, TOK), 0) < iota((TOK, TOK), 1), 1.0, 0.0).astype(jnp.bfloat16)
    place = nn(named.astype(jnp.bfloat16), earlier)
    place = jnp.where(named > 0.0, place, -1000.0)
    here = zh * 2 + c
    info[here, pl.ds(0, 16), :] = place
    info[here, pl.ds(16, 16), :] = weight

    partner = (zl * 4 + y + 1 - 2 * par, e)
    mine_at = pl.ds(pl.multiple_of(par * SHARE, 16), SHARE)
    other_at = pl.ds(pl.multiple_of((1 - par) * SHARE, 16), SHARE)
    inp[...] = inputs
    both[mine_at, :] = inputs
    own_lanes = pl.ds(pl.multiple_of(c * TOK, 128), TOK)
    toks[zh, pl.ds(pl.multiple_of(d * SHARE, 16), SHARE), own_lanes] = ct[...]

    def cot_copy(j):
        ref = toks.at[zh, pl.ds(pl.multiple_of(d * SHARE, 16), SHARE), own_lanes]
        return remote(ref, ref, cy_send.at[j - 1], cy_recv.at[j - 1], at_y(j))

    def info_copy(j):
        to = x * 4 + lax.rem(zh + j // 2, 2) * 2 + lax.rem(c + j, 2)
        return remote(info.at[here], info.at[here], info_send.at[j - 1], info_recv.at[j - 1], (d, to))

    pl.semaphore_wait(bar, 23)
    for j in (1, 2, 3):
        cot_copy(j).start()
    for j in (1, 2, 3):
        info_copy(j).start()
    swap = remote(inp, both.at[mine_at], swap_sem.at[0], swap_sem.at[1], partner)
    swap.start()

    slots = iota((SLOT, TOK), 0).astype(jnp.float32)
    for r in range(16):
        chosen = place[r : r + 1, :] == slots
        pick[pl.ds(r * SLOT, SLOT), :] = jnp.where(chosen, 1.0, 0.0).astype(jnp.bfloat16)
    dense = iota((QTR, 4 * SLOT), 0)
    squeeze[...] = jnp.where(
        iota((QTR, 4 * SLOT), 1) == dense + over_cap(dense) * (SLOT - CAP), 1.0, 0.0
    ).astype(jnp.bfloat16)

    def tok_block(o, half=None):
        src = lax.rem(z8 - o + 8, 8)
        low, count = (0, ZCOL) if half is None else (half * BLK, BLK)
        return toks.at[src // 4, pl.ds(pl.multiple_of(lax.rem(src, 4) * ZCOL + low, 16), count), own_lanes]

    def ring_copy(k, way):
        o = k - 1 if way == 0 else lax.rem(9 - k, 8)
        if k == 4:
            ref = tok_block(o, way)
        else:
            ref = tok_block(o)
        return remote(ref, ref, ring_send.at[way, k - 1], ring_recv.at[way, k - 1], at_ring(1 if way == 0 else 7))

    def ring_arrival(k, way):
        o = k if way == 0 else 8 - k
        if k == 4:
            ref = tok_block(o, way)
        else:
            ref = tok_block(o)
        return remote(ref, ref, ring_send.at[way, k - 1], ring_recv.at[way, k - 1], at_ring(1 if way == 0 else 7))

    def sib_copy(o):
        ref = tok_block(o)
        return remote(ref, ref, sib_send.at[o], sib_recv.at[o], (d, e + 1 - 2 * c))

    for j in (1, 2, 3):
        cot_copy(j).wait_recv()
    for way in (0, 1):
        ring_copy(1, way).start()
    sib_copy(0).start()

    def make_picks(hi):
        packed = iota((PACK, TOK), 0).astype(jnp.float32)
        for core in range(2):
            for to in range(4):
                row = zh * 8 + c * 4 + to
                chosen = info[hi * 2 + core, pl.ds(row, 1), :] + float(CAP * core) == packed
                pick_s[hi, pl.ds(to * PACK, PACK), pl.ds(core * TOK, TOK)] = jnp.where(
                    chosen, info[hi * 2 + core, pl.ds(row + 16, 1), :], 0.0
                ).astype(jnp.bfloat16)

    def s_rows(src, who, count):
        return pl.ds(pl.multiple_of(src // 4 * SIDE + who * PACK, 16), count)

    def s_cols(src):
        return pl.ds(pl.multiple_of(lax.rem(src, 4) * ZCOL, 128), ZCOL)

    def sx_copy(o, j):
        src = lax.rem(z8 - o + 8, 8)
        to = lax.rem(x + j, 4)
        return remote(sp.at[s_rows(src, to, PACK), s_cols(src)], ss.at[s_rows(src, x, PACK), s_cols(src)],
                      sx_send.at[o, j - 1], sx_recv.at[o, j - 1], (d, to * 4 + zh * 2 + c))

    def pick_chunk(o):
        sib_copy(o).wait_recv()
        src = lax.rem(z8 - o + 8, 8)
        sp[s_rows(src, 0, SIDE), s_cols(src)] = nt(pick_s[src // 4], toks[src // 4, s_cols(src), :]).astype(jnp.bfloat16)
        for j in (1, 3, 2):
            sx_copy(o, j).start()
        ss[s_rows(src, x, PACK), s_cols(src)] = sp[s_rows(src, x, PACK), s_cols(src)]

    def ring_step(k):
        for way in (0, 1):
            ring_arrival(k, way).wait_recv()
            if k < 4:
                ring_copy(k + 1, way).start()
        sib_copy(k).start()
        if k < 4:
            sib_copy(8 - k).start()
        pick_chunk(k)
        if k < 4:
            pick_chunk(8 - k)

    def offset_of(m):
        return jnp.where(lax.rem(m, 2) == 1, (m + 1) // 2, lax.rem(8 - m // 2, 8))

    def s_chunk(m):
        o = offset_of(m)
        src = lax.rem(z8 - o + 8, 8)
        for j in (1, 2, 3):
            sx_copy(o, j).wait_recv()
        rows = s_rows(src, 0, SIDE)
        acc_h[rows, :] += nt(ss[rows, s_cols(src)], w3[:, s_cols(src)])

    swap.wait()

    @pl.when(c == par)
    def _():
        picked = nt(pick[...], both[...]).astype(jnp.bfloat16)
        for r in range(16):
            sendb[r] = picked[r * SLOT : (r + 1) * SLOT]

    def slot_at(r):
        return r // 8 * 4 + lax.rem(r, 4)

    def dispatch(r):
        return remote(sendb.at[r], recvb.at[slot_at(rank)], disp_send.at[r], disp_recv.at[rank], (d, expert_of(r)))

    def arrival(r):
        return remote(sendb.at[rank], recvb.at[slot_at(r)], disp_send.at[rank], disp_recv.at[r], (d, expert_of(r)))

    @pl.when(c == par)
    def _():
        @pl.loop(0, 16)
        def _(i):
            r = lax.rem(i + 8 + zh * 8, 16)

            @pl.when(r != rank)
            def _():
                dispatch(r).start()

        recvb[slot_at(rank)] = sendb[rank]

    info_copy(1).wait_recv()
    make_picks(zh)
    pick_chunk(0)
    for j in (2, 3):
        info_copy(j).wait_recv()
    make_picks(1 - zh)
    dense = iota((4 * SLOT, QTR), 1)
    spread[...] = jnp.where(
        iota((4 * SLOT, QTR), 0) == dense + over_cap(dense) * (SLOT - CAP), 1.0, 0.0
    ).astype(jnp.bfloat16)
    dense = iota((HALF, SIDE), 0)
    which = over_cap(dense)
    perm[...] = jnp.where(
        iota((HALF, SIDE), 1) == (which & 3) * PACK + (which >> 2) * CAP + dense - which * CAP, 1.0, 0.0
    ).astype(jnp.bfloat16)
    row_of[...] = jnp.where(over_cap(iota((8, HALF), 1)) == iota((8, HALF), 0), 1.0, 0.0)
    dense = iota((HALF, 128), 0)
    slot_of[...] = jnp.where(dense - over_cap(dense) * CAP == iota((HALF, 128), 1), 1.0, 0.0)
    for h in (0, 1):
        pick_t[h] = pick[pl.ds(h * 8 * SLOT, 8 * SLOT), :].T
    w2[pl.ds(HID, HPAD - HID), :] = jnp.zeros((HPAD - HID, FEAT), jnp.bfloat16)
    w2[pl.ds(HPAD + HID, HPAD - HID), :] = jnp.zeros((HPAD - HID, FEAT), jnp.bfloat16)
    w3[pl.ds(HID, HPAD - HID), :] = jnp.zeros((HPAD - HID, FEAT), jnp.bfloat16)
    acc_gu[...] = jnp.zeros_like(acc_gu)
    acc_h[...] = jnp.zeros_like(acc_h)

    def block(h, z, yy, lo=0, rows=QTR):
        return xs.at[pl.ds(pl.multiple_of(h * HALF + lax.rem(yy, 2) * QTR + lo, 16), rows),
                     pl.ds(pl.multiple_of(z * ZCOL + yy // 2 * BLK, 128), BLK)]

    def z_copy(h, z, way):
        ref = block(h, z, y)
        return remote(ref, ref, gz_send.at[h * 4 + z, way], gz_recv.at[h * 4 + z], at_z(zl + 1 - 2 * way))

    def z_arrival(h, z):
        ref = block(h, z, y)
        return remote(ref, ref, gz_send.at[h * 4 + z, 0], gz_recv.at[h * 4 + z], at_z(lax.rem(zl + 1, 4)))

    def z_each(h, z, what):
        @pl.when(jnp.logical_and(z <= zl, zl < 3))
        def _():
            what(z_copy(h, z, 0))

        @pl.when(jnp.logical_and(z >= zl, zl > 0))
        def _():
            what(z_copy(h, z, 1))

    def take_half(h):
        @pl.loop(0, 4)
        def _(k):
            r = h * 8 + par * 4 + k

            @pl.when(r != rank)
            def _():
                arrival(r).wait_recv()

        slabs = recvb[pl.ds(h * 4, 4)].reshape(4 * SLOT, BLK)
        xs[pl.ds(pl.multiple_of(h * HALF + par * QTR, 16), QTR),
           pl.ds(pl.multiple_of(zl * ZCOL + sub * BLK, 128), BLK)] = nn(squeeze[...], slabs).astype(jnp.bfloat16)
        z_each(h, zl, lambda copy: copy.start())

    def chunk(s):
        i, j = s // 4, lax.rem(s, 4)
        h = lax.rem(zh + i, 2)
        first, second, third = zl + 1 - 2 * (zl // 2), lax.rem(2 + 3 * zl, 5), 3 - 3 * (zl // 2)
        z = jnp.where(j == 0, zl, jnp.where(j == 1, first, jnp.where(j == 2, second, third)))
        return h, j, z

    left, right = lax.rem(y + 3, 4), lax.rem(y + 1, 4)
    across = lax.rem(y + 2, 4)

    def y_copy(s, way):
        h, j, z = chunk(s)
        ref = block(h, z, y)
        return remote(ref, ref, gy_send.at[s, way], gy_recv.at[s, way], at_y(1 if way == 0 else 3))

    def y_arrival(s, way):
        h, j, z = chunk(s)
        ref = block(h, z, left if way == 0 else right)
        return remote(ref, ref, gy_send.at[s, way], gy_recv.at[s, way], at_y(1 if way == 0 else 3))

    CUT = ((0, 80), (80, 64))

    def turn(n, way):
        return 1 + 2 * lax.rem(n + way, 2)

    def d_copy(s, way):
        h, j, z = chunk(s)
        ref = block(h, z, lax.rem(y + 4 - turn(s, way), 4), *CUT[way])
        return remote(ref, ref, gd_send.at[s, way], gd_recv.at[s, way], at_y(turn(s, way)))

    def d_arrival(s, way):
        h, j, z = chunk(s)
        ref = block(h, z, across, *CUT[way])
        return remote(ref, ref, gd_send.at[s, way], gd_recv.at[s, way], at_y(turn(s, way)))

    def spread_chunk(s):
        h, j, z = chunk(s)

        @pl.when(j > 0)
        def _():
            z_arrival(h, z).wait_recv()
            z_each(h, z, lambda copy: copy.start())

        y_copy(s, 0).start()
        y_copy(s, 1).start()

    take_half(zh)
    spread_chunk(0)
    ring_step(1)
    spread_chunk(1)
    for load in loads:
        load.wait()

    @pl.loop(0, 9)
    def _(s):
        @pl.when(s == 2)
        def _():
            take_half(1 - zh)

        @pl.when(s < 6)
        def _():
            spread_chunk(s + 2)

        @pl.when(s < 8)
        def _():
            for way in (0, 1):
                y_arrival(s, way).wait_recv()
            for way in (0, 1):
                d_copy(s, way).start()

        for k in (2, 3, 4):
            @pl.when(s == k - 2)
            def _(k=k):
                ring_step(k)


        @pl.when(s > 0)
        def _():
            for way in (0, 1):
                d_arrival(s - 1, way).wait_recv()
            h, j, z = chunk(s - 1)
            rows = pl.ds(pl.multiple_of(h * HALF, 16), HALF)
            cols = pl.ds(pl.multiple_of(z * ZCOL, 128), ZCOL)
            acc_gu[rows, :] += nt(xs[rows, cols], w2[:, cols])

            @pl.when(j == 3)
            def _():
                @pl.loop(0, HALF // 32)
                def _(b):
                    part_rows = pl.ds(pl.multiple_of(h * HALF + b * 32, 16), 32)
                    gate = acc_gu[part_rows, pl.ds(0, HPAD)]
                    upper = acc_gu[part_rows, pl.ds(HPAD, HPAD)]
                    sig = jax.nn.sigmoid(gate)
                    swished = gate * sig
                    hidden[part_rows, :] = (swished * upper).astype(jnp.bfloat16)
                    acc_gu[part_rows, pl.ds(0, HPAD)] = upper * sig * (1.0 + gate * (1.0 - sig))
                    acc_gu[part_rows, pl.ds(HPAD, HPAD)] = swished

        @pl.when(s > 2)
        def _():
            s_chunk(s - 3)

    for h in (0, 1):
        hidden_t[:, pl.ds(h * SIDE, SIDE)] = nn(hidden[pl.ds(h * HALF, HALF), :].T, perm[...]).astype(jnp.bfloat16)
    s_chunk(6)
    s_chunk(7)

    def finish_half(h):
        grad = acc_h[pl.ds(pl.multiple_of(h * SIDE, 16), SIDE), :]
        high = grad.astype(jnp.bfloat16)
        low = (grad - high.astype(jnp.float32)).astype(jnp.bfloat16)
        grad_x[...] = nn(perm[...], high) + nn(perm[...], low)

        @pl.loop(0, HALF // 32)
        def _(b):
            part_rows = pl.ds(pl.multiple_of(h * HALF + b * 32, 16), 32)
            grad = grad_x[pl.ds(pl.multiple_of(b * 32, 16), 32), :]
            hid[part_rows, pl.ds(0, HPAD)] = (grad * acc_gu[part_rows, pl.ds(0, HPAD)]).astype(jnp.bfloat16)
            hid[part_rows, pl.ds(HPAD, HPAD)] = (grad * acc_gu[part_rows, pl.ds(HPAD, HPAD)]).astype(jnp.bfloat16)
            total = jnp.sum(hidden[part_rows, :].astype(jnp.float32) * grad, axis=1, keepdims=True)
            prob[part_rows, :] = jnp.broadcast_to(total, (32, 128))

    def p_y(j):
        return remote(pbuf, py.at[j - 1], p_send.at[j - 1], p_recv.at[j - 1], at_y(j))

    def p_z(j):
        return remote(pz.at[3], pz.at[j - 1], p_send.at[2 + j], p_recv.at[2 + j], at_z(lax.rem(zl + j, 4)))

    def p_b(step):
        return remote(ptot, back.at[rank], pb_send.at[step], pb_recv.at[rank],
                      (d, lax.rem(e + step, 16)))

    def rs_step(n):
        i, q = n // 4, lax.rem(n, 4)
        return lax.rem(zh + 1 + i, 2), lax.rem(zl + 1 + q, 4)

    def piece(yy, n, lo, rows):
        h, z = rs_step(n)
        return (pl.ds(pl.multiple_of(h * HALF + lax.rem(yy, 2) * QTR + lo, 16), rows),
                pl.ds(pl.multiple_of(z * ZCOL + yy // 2 * BLK, 128), BLK))

    def diag_copy(n, way):
        lo, rows = CUT[way]
        return remote(part.at[piece(across, n, lo, rows)], diag.at[n, pl.ds(lo, rows)],
                      rd_send.at[n, way], rd_recv.at[n, way], at_y(turn(n, way)))

    def own_copy(n, way):
        lo, rows = CUT[1 - way]
        to = lax.rem(y + turn(n, way), 4)
        return remote(part.at[piece(to, n, lo, rows)], ybuf.at[n, way, pl.ds(lo, rows)],
                      ro_send.at[n, way], ro_recv.at[n, way], at_y(turn(n, way)))

    def sum_copy(n, way):
        lo, rows = CUT[way]
        return remote(dsum.at[n, pl.ds(lo, rows)], ybuf.at[n, way, pl.ds(lo, rows)],
                      rs_send.at[n, way], rs_recv.at[n, way], at_y(turn(n, way)))

    def zred_copy(n):
        return remote(zsend.at[n], zrecv.at[n], rz_send.at[n], rz_recv.at[n], at_z(rs_step(n)[1]))

    def make_part(n):
        h, z = rs_step(n)
        rows = pl.ds(pl.multiple_of(h * HALF, 16), HALF)
        cols = pl.ds(pl.multiple_of(z * ZCOL, 128), ZCOL)
        part[rows, cols] = nn(hid[rows, :], w2[:, cols]).astype(jnp.bfloat16)
        for way in (0, 1):
            diag_copy(n, way).start()
        for way in (0, 1):
            own_copy(n, way).start()

    def out_copies(q):
        cols = pl.ds(pl.multiple_of(q * ZCOL, 128), ZCOL)
        return (
            pltpu.make_async_copy(ogu.at[pl.ds(0, HID), cols], gg_out.at[:, cols], out_sem.at[q, 0]),
            pltpu.make_async_copy(ogu.at[pl.ds(HPAD, HID), cols], gu_out.at[:, cols], out_sem.at[q, 1]),
            pltpu.make_async_copy(ogd.at[pl.ds(0, HID), cols], gd_out.at[:, cols], out_sem.at[q, 2]),
        )

    def weight_grads(q):
        cols = pl.ds(pl.multiple_of(q * ZCOL, 128), ZCOL)
        ogu[:, cols] = nn(hid_t[...], xs[:, cols]).astype(jnp.bfloat16)
        ogd[:, cols] = nn(hidden_t[...], ss[:, cols]).astype(jnp.bfloat16)
        for out in out_copies(q):
            out.start()

    def y_sum(n):
        for way in (0, 1):
            own_copy(n, way).wait_recv()
            sum_copy(n, way).wait_recv()
        own = part[piece(y, n, 0, QTR)].astype(jnp.float32)
        return own + (ybuf[n, 0].astype(jnp.float32) + ybuf[n, 1].astype(jnp.float32))

    def ret_rank(i, k):
        return lax.rem(zh + 1 + i, 2) * 8 + par * 4 + k

    def ret_copy(i, k):
        return remote(retsend.at[i * 4 + k], retrecv.at[rank], ret_send.at[i * 4 + k], ret_recv.at[rank],
                      (d, expert_of(ret_rank(i, k))))

    def ret_arrival(r):
        return remote(retsend.at[0], retrecv.at[r], ret_send.at[0], ret_recv.at[r], (d, expert_of(r)))

    def send_back(i):
        total = y_sum(i * 4 + 3)
        for q in range(3):
            zred_copy(i * 4 + q).wait_recv()
            total += zrecv[i * 4 + q].astype(jnp.float32)
        slabs = nn(spread[...], total.astype(jnp.bfloat16)).astype(jnp.bfloat16)
        for k in range(4):
            retsend[i * 4 + k] = slabs[k * SLOT : (k + 1) * SLOT]
            if i == 0:
                ret_copy(i, k).start()
            else:
                @pl.when(ret_rank(i, k) != rank)
                def _(k=k):
                    ret_copy(i, k).start()

                @pl.when(ret_rank(i, k) == rank)
                def _(k=k):
                    retrecv[rank] = slabs[k * SLOT : (k + 1) * SLOT]

    finish_half(1 - zh)
    make_part(0)
    make_part(1)
    finish_half(zh)
    for h in (0, 1):
        pbuf[pl.ds(h * 8, 8), :] = jnp.dot(
            row_of[...], prob[pl.ds(h * HALF, HALF), :] * slot_of[...],
            precision=lax.Precision.HIGHEST, preferred_element_type=jnp.float32,
        )

    for j in (1, 2, 3):
        p_y(j).start()
    hid_t[...] = hid[...].T

    @pl.loop(0, 8)
    def _(n):
        @pl.when(n < 6)
        def _():
            make_part(n + 2)

        for way in (0, 1):
            diag_copy(n, way).wait_recv()
            lo, rows = CUT[way]
            to = lax.rem(y + turn(n, way), 4)
            dsum[n, pl.ds(lo, rows)] = (
                part[piece(to, n, lo, rows)].astype(jnp.float32)
                + diag[n, pl.ds(lo, rows)].astype(jnp.float32)
            ).astype(jnp.bfloat16)
            sum_copy(n, way).start()

        @pl.when(n < 4)
        def _():
            weight_grads(n)

        @pl.when(n == 1)
        def _():
            for j in (1, 2, 3):
                p_y(j).wait_recv()
            pz[3] = pbuf[...] + py[0] + py[1] + py[2]
            for j in (1, 2, 3):
                p_z(j).start()

        @pl.when(n == 3)
        def _():
            for j in (1, 2, 3):
                p_z(j).wait_recv()
            ptot[...] = pz[0] + pz[1] + pz[2] + pz[3]
            back[rank] = ptot[...]

            @pl.loop(1, 16)
            def _(step):
                p_b(step).start()

        @pl.when(jnp.logical_and(n > 0, n != 4))
        def _():
            zsend[n - 1] = y_sum(n - 1).astype(jnp.bfloat16)
            zred_copy(n - 1).start()

        @pl.when(n == 4)
        def _():
            send_back(0)

    send_back(1)

    @pl.loop(0, 16)
    def _(r):
        @pl.when(r != rank)
        def _():
            remote(ptot, back.at[r], pb_send.at[0], pb_recv.at[r], (d, expert_of(r))).wait_recv()

    own = jnp.concatenate([back[r, pl.ds(rank, 1), :] for r in range(16)], axis=0)
    own_t = jnp.concatenate([own, jnp.zeros((112, 128), jnp.float32)], axis=0).T
    per_expert = jnp.concatenate(
        [
            jnp.sum(pick[pl.ds(r * SLOT, SLOT), :].astype(jnp.float32) * own_t[:SLOT, r : r + 1],
                    axis=0, keepdims=True)
            for r in range(16)
        ],
        axis=0,
    )
    grads = [
        jnp.sum(jnp.where(ids[pl.ds(k, 1), :] == expert, per_expert, 0.0), axis=0, keepdims=True)
        for k in range(4)
    ]
    droute[...] = (jnp.concatenate(grads, axis=0) / wts[...].astype(jnp.float32)).astype(jnp.bfloat16)

    fin = remote(res.at[other_at], res.at[other_at], fin_sem.at[0], fin_sem.at[1], partner)

    @pl.when(c == par)
    def _():
        def from_half(h):
            @pl.loop(0, 8)
            def _(k):
                @pl.when(h * 8 + k != rank)
                def _():
                    ret_arrival(h * 8 + k).wait_recv()

            return nn(pick_t[h], retrecv[pl.ds(h * 8, 8)].reshape(8 * SLOT, BLK))

        total = from_half(1 - zh)
        total += from_half(zh)
        res[...] = total.T.astype(jnp.bfloat16)
        fin.start()
        fin.wait_send()

    @pl.when(c != par)
    def _():
        fin.wait_recv()

    dv[...] = (res[mine_at, :].astype(jnp.float32) * factor[...]).astype(jnp.bfloat16)

    @pl.loop(0, 16)
    def _(r):
        @pl.when(jnp.logical_and(r != rank, c == par))
        def _():
            dispatch(r).wait_send()

    for j in (1, 2, 3):
        cot_copy(j).wait_send()
        info_copy(j).wait_send()
    for k in (1, 2, 3, 4):
        for way in (0, 1):
            ring_copy(k, way).wait_send()

    @pl.loop(0, 8)
    def _(o):
        sib_copy(o).wait_send()
        for j in (1, 2, 3):
            sx_copy(o, j).wait_send()

    @pl.loop(1, 16)
    def _(step):
        p_b(step).wait_send()

    for k in range(4):
        ret_copy(0, k).wait_send()

        @pl.when(ret_rank(1, k) != rank)
        def _(k=k):
            ret_copy(1, k).wait_send()

    @pl.loop(0, 8)
    def _(s):
        for way in (0, 1):
            y_copy(s, way).wait_send()
            d_copy(s, way).wait_send()
            diag_copy(s, way).wait_send()
            own_copy(s, way).wait_send()
            sum_copy(s, way).wait_send()

    @pl.loop(0, 8)
    def _(s):
        z_each(s // 4, lax.rem(s, 4), lambda copy: copy.wait_send())

    for j in (1, 2, 3):
        p_y(j).wait_send()
        p_z(j).wait_send()

    @pl.loop(0, 4)
    def _(q):
        for out in out_copies(q):
            out.wait()

    for q in range(3):
        zred_copy(q).wait_send()
        zred_copy(4 + q).wait_send()


def finish(dv_in, droute_in, gg_in, gu_in, gd_in, dv, droute, gg, gu, gd, small, tiny, held, in_sem, out_sem):
    trips = [(dv_in, small, dv), (droute_in, tiny, droute)]
    for i, (src, dst) in enumerate(((gg_in, gg), (gu_in, gu), (gd_in, gd))):
        for part in range(3):
            rows = pl.ds(part * 112, 112)
            trips.append((src.at[rows], held.at[i, rows], dst.at[rows]))
    loads = [pltpu.make_async_copy(src, mid, in_sem.at[i]) for i, (src, mid, _) in enumerate(trips)]
    stores = [pltpu.make_async_copy(mid, dst, out_sem.at[i]) for i, (_, mid, dst) in enumerate(trips)]
    for load in loads:
        load.start()
    for load, store in zip(loads, stores):
        load.wait()
        store.start()
    for store in stores:
        store.wait()


def on_device(values, exponents, expert_ids, route_weights, cotangent, w_gate, w_up, w_down):
    vmem, hbm = pl.BlockSpec(memory_space=pltpu.VMEM), pl.BlockSpec(memory_space=pl.ANY)
    dma = pltpu.SemaphoreType.DMA
    bf, f32 = jnp.bfloat16, jnp.float32
    grad = jax.ShapeDtypeStruct((HID, FEAT), bf)
    outs = pl.pallas_call(
        kernel,
        out_shape=(
            jax.ShapeDtypeStruct((SHARE, TOK), bf),
            jax.ShapeDtypeStruct((4, TOK), bf),
            grad, grad, grad,
        ),
        in_specs=[vmem] * 5 + [hbm] * 3,
        out_specs=(vmem, vmem, hbm, hbm, hbm),
        scratch_shapes=[
            pltpu.VMEM((SHARE, TOK), bf),
            pltpu.VMEM((BLK, TOK), bf),
            pltpu.VMEM((SHARE, TOK), f32),
            pltpu.VMEM((16 * SLOT, TOK), bf),
            pltpu.VMEM((2, TOK, 8 * SLOT), bf),
            pltpu.VMEM((2, SIDE, 2 * TOK), bf),
            pltpu.VMEM((QTR, 4 * SLOT), bf),
            pltpu.VMEM((4 * SLOT, QTR), bf),
            pltpu.VMEM((HALF, SIDE), bf),
            pltpu.VMEM((8, HALF), f32),
            pltpu.VMEM((HALF, 128), f32),
            pltpu.VMEM((16, 16, 128), f32),
            pltpu.VMEM((BLK, TOK), bf),
            pltpu.VMEM((4, 32, TOK), f32),
            pltpu.VMEM((2, FEAT, 2 * TOK), bf),
            pltpu.VMEM((2 * SIDE, FEAT), bf),
            pltpu.VMEM((16, SLOT, BLK), bf),
            pltpu.VMEM((8, SLOT, BLK), bf),
            pltpu.VMEM((ROWS, FEAT), bf),
            pltpu.VMEM((2 * SIDE, FEAT), bf),
            pltpu.VMEM((2 * HPAD, FEAT), bf),
            pltpu.VMEM((HPAD, FEAT), bf),
            pltpu.VMEM((ROWS, 2 * HPAD), f32),
            pltpu.VMEM((2 * SIDE, HPAD), f32),
            pltpu.VMEM((HALF, HPAD), f32),
            pltpu.VMEM((ROWS, 2 * HPAD), bf),
            pltpu.VMEM((ROWS, HPAD), bf),
            pltpu.VMEM((2 * HPAD, ROWS), bf),
            pltpu.VMEM((HPAD, 2 * SIDE), bf),
            pltpu.VMEM((ROWS, 128), f32),
            pltpu.VMEM((ROWS, FEAT), bf),
            pltpu.VMEM((8, QTR, BLK), bf),
            pltpu.VMEM((8, QTR, BLK), bf),
            pltpu.VMEM((8, 2, QTR, BLK), bf),
            pltpu.VMEM((8, QTR, BLK), bf),
            pltpu.VMEM((8, QTR, BLK), bf),
            pltpu.VMEM((8, SLOT, BLK), bf),
            pltpu.VMEM((16, SLOT, BLK), bf),
            pltpu.VMEM((16, 128), f32),
            pltpu.VMEM((3, 16, 128), f32),
            pltpu.VMEM((4, 16, 128), f32),
            pltpu.VMEM((16, 128), f32),
            pltpu.VMEM((2 * HPAD, FEAT), bf),
            pltpu.VMEM((HPAD, FEAT), bf),
            dma((2,)), dma((16,)), dma((16,)), dma((3,)),
            dma((8, 2)), dma((8,)), dma((8, 2)), dma((8, 2)), dma((8, 2)), dma((8, 2)),
            dma((3,)), dma((3,)), dma((3,)), dma((3,)), dma((2, 4)), dma((2, 4)), dma((8,)), dma((8,)),
            dma((8, 3)), dma((8, 3)),
            dma((8, 2)), dma((8, 2)), dma((8, 2)), dma((8, 2)), dma((8, 2)), dma((8, 2)),
            dma((8,)), dma((8,)),
            dma((8,)), dma((16,)), dma((2,)), dma((6,)), dma((6,)), dma((16,)), dma((16,)),
            dma((4, 3)),
        ],
        compiler_params=pltpu.CompilerParams(
            collective_id=1, has_side_effects=True, vmem_limit_bytes=56 << 20
        ),
        name="moe_backward",
    )(values.T, cotangent.T, exponents.T, expert_ids.T, route_weights.T, w_gate[0], w_up[0], w_down[0])
    dv, droute, gg, gu, gd = pl.pallas_call(
        finish,
        out_shape=[jax.ShapeDtypeStruct(out.shape, bf) for out in outs],
        in_specs=[hbm] * 5,
        out_specs=[hbm] * 5,
        scratch_shapes=[
            pltpu.VMEM((SHARE, TOK), bf),
            pltpu.VMEM((4, TOK), bf),
            pltpu.VMEM((3, HID, FEAT), bf),
            dma((11,)), dma((11,)),
        ],
        cost_estimate=pl.CostEstimate(flops=0, bytes_accessed=12 << 20, transcendentals=0),
        name="finish",
    )(*outs)
    return dv.T, droute.T, gg[None], gu[None], gd[None]


def solution(mesh):
    in_specs = (
        P("expert", "dp"),
        P("expert", None),
        P("expert", None),
        P("expert", None),
        P("expert", "dp"),
        P("expert", "dp", None),
        P("expert", "dp", None),
        P("expert", "dp", None),
    )
    out_specs = (
        P("expert", "dp"),
        P("expert", None),
        P("expert", "dp", None),
        P("expert", "dp", None),
        P("expert", "dp", None),
    )
    return jax.shard_map(
        on_device, mesh=mesh, in_specs=in_specs, out_specs=out_specs, check_vma=False
    )
```

```python
import functools

import jax
import jax.numpy as jnp
from jax import lax
from jax.experimental import pallas as pl
from jax.experimental.pallas import tpu as pltpu
from jax.sharding import PartitionSpec as P

MESH = pl.DeviceIdType.MESH

SLOT = 48
CAP = 36
TOK = 128
BLK = 384
WIDE = 256
ZCOL = 2 * BLK
SHARE = 192
HID = 336
HPAD = 384
FEAT = 3072
ROWS = 16 * CAP
HALF = ROWS // 2
QTR = HALF // 2
PACK = 80
SIDE = 4 * PACK


def nt(left, right):
    return lax.dot_general(left, right, (((1,), (1,)), ((), ())), preferred_element_type=jnp.float32)


def tn(left, right):
    return lax.dot_general(left, right, (((0,), (0,)), ((), ())), preferred_element_type=jnp.float32)


def nn(left, right):
    return jnp.dot(left, right, preferred_element_type=jnp.float32)


def iota(shape, axis):
    return lax.broadcasted_iota(jnp.int32, shape, axis)


def over_cap(number):
    return (number * 1821) >> 16


def kernel(
    vt, ct, exps, ids, wts, wg, wu, wd,
    dv, droute, gg_out, gu_out, gd_out,
    inp, both, factor, pick, pick_t, pick_s, squeeze, spread, perm, row_of, slot_of, back, res, info, toks, sp,
    sendb, recvb, xs, ss, w2, w3, acc_gu, acc_h, grad_x, hid, hidden, hid_t, hidden_t, prob, part,
    diag, dsum, ybuf, zsend, zrecv, retsend, retrecv, pbuf, py, pz, ptot, ogu, ogd,
    swap_sem, disp_send, disp_recv, w_sem, gz_send, gz_recv, gy_send, gy_recv, gd_send, gd_recv,
    info_send, info_recv, cy_send, cy_recv, ring_send, ring_recv, sib_send, sib_recv, sx_send, sx_recv,
    rd_send, rd_recv, ro_send, ro_recv, rs_send, rs_recv, rz_send, rz_recv,
    ret_send, ret_recv, p_send, p_recv, pb_send, pb_recv, out_sem,
):
    d = lax.axis_index("dp")
    e = lax.axis_index("expert")
    y, zl = lax.rem(d, 4), d // 4
    par, sub = lax.rem(y, 2), y // 2
    x, zh, c = e // 4, lax.rem(e // 2, 2), lax.rem(e, 2)
    rank = zh * 8 + c * 4 + x
    z8 = zh * 4 + zl

    def at_y(step):
        return (zl * 4 + lax.rem(y + step + 4, 4), e)

    def at_z(z):
        return (z * 4 + y, e)

    def at_ring(step):
        to = lax.rem(z8 + step + 8, 8)
        return (lax.rem(to, 4) * 4 + y, x * 4 + to // 4 * 2 + c)

    def expert_of(r):
        return lax.rem(r, 4) * 4 + r // 8 * 2 + lax.rem(r, 8) // 4

    def remote(src, dst, ssem, rsem, dev):
        return pltpu.make_async_remote_copy(src, dst, ssem, rsem, device_id=dev, device_id_type=MESH)

    bar = pltpu.get_barrier_semaphore()
    for step in (1, 2, 3):
        pl.semaphore_signal(bar, inc=1, device_id=at_y(step), device_id_type=MESH)
        pl.semaphore_signal(bar, inc=1, device_id=at_z(lax.rem(zl + step, 4)), device_id_type=MESH)
    for step in range(1, 16):
        pl.semaphore_signal(bar, inc=1, device_id=(d, lax.rem(e + step, 16)), device_id_type=MESH)

    for step in (1, 7):
        pl.semaphore_signal(bar, inc=1, device_id=at_ring(step), device_id_type=MESH)

    @pl.when(c != par)
    def _():
        for to in range(16):
            pl.semaphore_signal(bar, inc=1, device_id=(d + 1 - 2 * par, to), device_id_type=MESH)

    loads = [
        pltpu.make_async_copy(wg, w2.at[pl.ds(0, HID)], w_sem.at[0]),
        pltpu.make_async_copy(wu, w2.at[pl.ds(HPAD, HID)], w_sem.at[1]),
        pltpu.make_async_copy(wd, w3.at[pl.ds(0, HID)], w_sem.at[2]),
    ]
    for load in loads:
        load.start()

    block_of = (d * SHARE + iota((SHARE, 24), 0)) >> 7
    block_map = (block_of == iota((SHARE, 24), 1)).astype(jnp.bfloat16)
    factor[...] = nn(block_map, jnp.exp2(exps[...].astype(jnp.float32)).astype(jnp.bfloat16))
    inputs = (vt[...].astype(jnp.float32) * factor[...]).astype(jnp.bfloat16)

    order = iota((16, TOK), 0)
    expert = (order & 3) * 4 + (order >> 3) * 2 + ((order >> 2) & 1)
    wide = wts[...].astype(jnp.float32)
    named = jnp.zeros((16, TOK), jnp.float32)
    weight = jnp.zeros((16, TOK), jnp.float32)
    for k in range(4):
        hit = ids[pl.ds(k, 1), :] == expert
        named += jnp.where(hit, 1.0, 0.0)
        weight += jnp.where(hit, wide[k : k + 1, :], 0.0)
    earlier = jnp.where(iota((TOK, TOK), 0) < iota((TOK, TOK), 1), 1.0, 0.0).astype(jnp.bfloat16)
    place = nn(named.astype(jnp.bfloat16), earlier)
    place = jnp.where(named > 0.0, place, -1000.0)
    here = zh * 2 + c
    info[here, pl.ds(0, 16), :] = place
    info[here, pl.ds(16, 16), :] = weight

    partner = (zl * 4 + y + 1 - 2 * par, e)
    mine_at = pl.ds(pl.multiple_of(par * SHARE, 16), SHARE)
    inp[...] = inputs
    both[mine_at, :] = inputs
    own_lanes = pl.ds(pl.multiple_of(c * TOK, 128), TOK)
    toks[zh, pl.ds(pl.multiple_of(d * SHARE, 16), SHARE), own_lanes] = ct[...]

    def cot_copy(j):
        ref = toks.at[zh, pl.ds(pl.multiple_of(d * SHARE, 16), SHARE), own_lanes]
        return remote(ref, ref, cy_send.at[j - 1], cy_recv.at[j - 1], at_y(j))

    def info_copy(j):
        to = x * 4 + lax.rem(zh + j // 2, 2) * 2 + lax.rem(c + j, 2)
        return remote(info.at[here], info.at[here], info_send.at[j - 1], info_recv.at[j - 1], (d, to))

    pl.semaphore_wait(bar, 31)
    for j in (1, 2, 3):
        cot_copy(j).start()
    for j in (1, 2, 3):
        info_copy(j).start()
    swap = remote(inp, both.at[mine_at], swap_sem.at[0], swap_sem.at[1], partner)
    swap.start()

    slots = iota((SLOT, TOK), 0).astype(jnp.float32)
    for r in range(16):
        chosen = place[r : r + 1, :] == slots
        pick[pl.ds(r * SLOT, SLOT), :] = jnp.where(chosen, 1.0, 0.0).astype(jnp.bfloat16)
    dense = iota((QTR, 4 * SLOT), 0)
    squeeze[...] = jnp.where(
        iota((QTR, 4 * SLOT), 1) == dense + over_cap(dense) * (SLOT - CAP), 1.0, 0.0
    ).astype(jnp.bfloat16)

    def tok_block(o, half=None):
        src = lax.rem(z8 - o + 8, 8)
        low, count = (0, ZCOL) if half is None else (half * BLK, BLK)
        return toks.at[src // 4, pl.ds(pl.multiple_of(lax.rem(src, 4) * ZCOL + low, 16), count), own_lanes]

    def ring_copy(k, way):
        o = k - 1 if way == 0 else lax.rem(9 - k, 8)
        if k == 4:
            ref = tok_block(o, way)
        else:
            ref = tok_block(o)
        return remote(ref, ref, ring_send.at[way, k - 1], ring_recv.at[way, k - 1], at_ring(1 if way == 0 else 7))

    def ring_arrival(k, way):
        o = k if way == 0 else 8 - k
        if k == 4:
            ref = tok_block(o, way)
        else:
            ref = tok_block(o)
        return remote(ref, ref, ring_send.at[way, k - 1], ring_recv.at[way, k - 1], at_ring(1 if way == 0 else 7))

    def sib_copy(o):
        ref = tok_block(o)
        return remote(ref, ref, sib_send.at[o], sib_recv.at[o], (d, e + 1 - 2 * c))

    for j in (1, 2, 3):
        cot_copy(j).wait_recv()
    for way in (0, 1):
        ring_copy(1, way).start()
    sib_copy(0).start()

    def make_picks(hi):
        packed = iota((PACK, TOK), 0).astype(jnp.float32)
        for core in range(2):
            for to in range(4):
                row = zh * 8 + c * 4 + to
                chosen = info[hi * 2 + core, pl.ds(row, 1), :] + float(CAP * core) == packed
                pick_s[hi, pl.ds(to * PACK, PACK), pl.ds(core * TOK, TOK)] = jnp.where(
                    chosen, info[hi * 2 + core, pl.ds(row + 16, 1), :], 0.0
                ).astype(jnp.bfloat16)

    def s_rows(src, who, count):
        return pl.ds(pl.multiple_of(src // 4 * SIDE + who * PACK, 16), count)

    def s_cols(src):
        return pl.ds(pl.multiple_of(lax.rem(src, 4) * ZCOL, 128), ZCOL)

    def sx_copy(o, j):
        src = lax.rem(z8 - o + 8, 8)
        to = lax.rem(x + j, 4)
        return remote(sp.at[s_rows(src, to, PACK), s_cols(src)], ss.at[s_rows(src, x, PACK), s_cols(src)],
                      sx_send.at[o, j - 1], sx_recv.at[o, j - 1], (d, to * 4 + zh * 2 + c))

    def pick_chunk(o):
        sib_copy(o).wait_recv()
        src = lax.rem(z8 - o + 8, 8)
        sp[s_rows(src, 0, SIDE), s_cols(src)] = nt(pick_s[src // 4], toks[src // 4, s_cols(src), :]).astype(jnp.bfloat16)
        for j in (1, 3, 2):
            sx_copy(o, j).start()
        ss[s_rows(src, x, PACK), s_cols(src)] = sp[s_rows(src, x, PACK), s_cols(src)]

    def ring_step(k):
        for way in (0, 1):
            ring_arrival(k, way).wait_recv()
            if k < 4:
                ring_copy(k + 1, way).start()
        sib_copy(k).start()
        if k < 4:
            sib_copy(8 - k).start()
        pick_chunk(k)
        if k < 4:
            pick_chunk(8 - k)

    def offset_of(m):
        return jnp.where(lax.rem(m, 2) == 1, (m + 1) // 2, lax.rem(8 - m // 2, 8))

    def s_chunk(m):
        o = offset_of(m)
        src = lax.rem(z8 - o + 8, 8)
        for j in (1, 2, 3):
            sx_copy(o, j).wait_recv()
        rows = s_rows(src, 0, SIDE)
        acc_h[rows, :] += nt(ss[rows, s_cols(src)], w3[:, s_cols(src)])

    swap.wait()

    @pl.when(c == par)
    def _():
        picked = nt(pick[...], both[...]).astype(jnp.bfloat16)
        for r in range(16):
            sendb[r] = picked[r * SLOT : (r + 1) * SLOT]

    def slot_at(r):
        return r // 8 * 4 + lax.rem(r, 4)

    def dispatch(r):
        return remote(sendb.at[r], recvb.at[slot_at(rank)], disp_send.at[r], disp_recv.at[rank], (d, expert_of(r)))

    def arrival(r):
        return remote(sendb.at[rank], recvb.at[slot_at(r)], disp_send.at[rank], disp_recv.at[r], (d, expert_of(r)))

    @pl.when(c == par)
    def _():
        @pl.loop(0, 16)
        def _(i):
            r = lax.rem(i + 8 + zh * 8, 16)

            @pl.when(r != rank)
            def _():
                dispatch(r).start()

        recvb[slot_at(rank)] = sendb[rank]

    info_copy(1).wait_recv()
    make_picks(zh)
    pick_chunk(0)
    for j in (2, 3):
        info_copy(j).wait_recv()
    make_picks(1 - zh)
    dense = iota((4 * SLOT, QTR), 1)
    spread[...] = jnp.where(
        iota((4 * SLOT, QTR), 0) == dense + over_cap(dense) * (SLOT - CAP), 1.0, 0.0
    ).astype(jnp.bfloat16)
    dense = iota((HALF, SIDE), 0)
    which = over_cap(dense)
    perm[...] = jnp.where(
        iota((HALF, SIDE), 1) == (which & 3) * PACK + (which >> 2) * CAP + dense - which * CAP, 1.0, 0.0
    ).astype(jnp.bfloat16)
    row_of[...] = jnp.where(over_cap(iota((8, HALF), 1)) == iota((8, HALF), 0), 1.0, 0.0)
    dense = iota((HALF, 128), 0)
    slot_of[...] = jnp.where(dense - over_cap(dense) * CAP == iota((HALF, 128), 1), 1.0, 0.0)
    for h in (0, 1):
        pick_t[h] = pick[pl.ds(h * 8 * SLOT, 8 * SLOT), :].T
    w2[pl.ds(HID, HPAD - HID), :] = jnp.zeros((HPAD - HID, FEAT), jnp.bfloat16)
    w2[pl.ds(HPAD + HID, HPAD - HID), :] = jnp.zeros((HPAD - HID, FEAT), jnp.bfloat16)
    w3[pl.ds(HID, HPAD - HID), :] = jnp.zeros((HPAD - HID, FEAT), jnp.bfloat16)
    acc_gu[...] = jnp.zeros_like(acc_gu)
    acc_h[...] = jnp.zeros_like(acc_h)

    def block(h, z, yy, lo=0, rows=QTR):
        return xs.at[pl.ds(pl.multiple_of(h * HALF + lax.rem(yy, 2) * QTR + lo, 16), rows),
                     pl.ds(pl.multiple_of(z * ZCOL + yy // 2 * BLK, 128), BLK)]

    def z_copy(h, z, way):
        ref = block(h, z, y)
        return remote(ref, ref, gz_send.at[h * 4 + z, way], gz_recv.at[h * 4 + z], at_z(zl + 1 - 2 * way))

    def z_arrival(h, z):
        ref = block(h, z, y)
        return remote(ref, ref, gz_send.at[h * 4 + z, 0], gz_recv.at[h * 4 + z], at_z(lax.rem(zl + 1, 4)))

    def z_each(h, z, what):
        @pl.when(jnp.logical_and(z <= zl, zl < 3))
        def _():
            what(z_copy(h, z, 0))

        @pl.when(jnp.logical_and(z >= zl, zl > 0))
        def _():
            what(z_copy(h, z, 1))

    def take_half(h):
        @pl.loop(0, 4)
        def _(k):
            r = h * 8 + par * 4 + k

            @pl.when(r != rank)
            def _():
                arrival(r).wait_recv()

        slabs = recvb[pl.ds(h * 4, 4)].reshape(4 * SLOT, BLK)
        xs[pl.ds(pl.multiple_of(h * HALF + par * QTR, 16), QTR),
           pl.ds(pl.multiple_of(zl * ZCOL + sub * BLK, 128), BLK)] = nn(squeeze[...], slabs).astype(jnp.bfloat16)
        z_each(h, zl, lambda copy: copy.start())

    def chunk(s):
        i, j = s // 4, lax.rem(s, 4)
        h = lax.rem(zh + i, 2)
        first, second, third = zl + 1 - 2 * (zl // 2), lax.rem(2 + 3 * zl, 5), 3 - 3 * (zl // 2)
        z = jnp.where(j == 0, zl, jnp.where(j == 1, first, jnp.where(j == 2, second, third)))
        return h, j, z

    left, right = lax.rem(y + 3, 4), lax.rem(y + 1, 4)
    across = lax.rem(y + 2, 4)

    def y_copy(s, way):
        h, j, z = chunk(s)
        ref = block(h, z, y)
        return remote(ref, ref, gy_send.at[s, way], gy_recv.at[s, way], at_y(1 if way == 0 else 3))

    def y_arrival(s, way):
        h, j, z = chunk(s)
        ref = block(h, z, left if way == 0 else right)
        return remote(ref, ref, gy_send.at[s, way], gy_recv.at[s, way], at_y(1 if way == 0 else 3))

    CUT = ((0, 80), (80, 64))

    def turn(n, way):
        return 1 + 2 * lax.rem(n + way, 2)

    def d_copy(s, way):
        h, j, z = chunk(s)
        ref = block(h, z, lax.rem(y + 4 - turn(s, way), 4), *CUT[way])
        return remote(ref, ref, gd_send.at[s, way], gd_recv.at[s, way], at_y(turn(s, way)))

    def d_arrival(s, way):
        h, j, z = chunk(s)
        ref = block(h, z, across, *CUT[way])
        return remote(ref, ref, gd_send.at[s, way], gd_recv.at[s, way], at_y(turn(s, way)))

    def spread_chunk(s):
        h, j, z = chunk(s)

        @pl.when(j > 0)
        def _():
            z_arrival(h, z).wait_recv()
            z_each(h, z, lambda copy: copy.start())

        y_copy(s, 0).start()
        y_copy(s, 1).start()

    take_half(zh)
    spread_chunk(0)
    spread_chunk(1)
    ring_step(1)
    for load in loads:
        load.wait()

    @pl.loop(0, 9)
    def _(s):
        @pl.when(s == 2)
        def _():
            take_half(1 - zh)

        @pl.when(s < 6)
        def _():
            spread_chunk(s + 2)

        @pl.when(s < 8)
        def _():
            for way in (0, 1):
                y_arrival(s, way).wait_recv()
            for way in (0, 1):
                d_copy(s, way).start()

        for k in (2, 3, 4):
            @pl.when(s == k - 2)
            def _(k=k):
                ring_step(k)


        @pl.when(s > 0)
        def _():
            for way in (0, 1):
                d_arrival(s - 1, way).wait_recv()
            h, j, z = chunk(s - 1)
            rows = pl.ds(pl.multiple_of(h * HALF, 16), HALF)
            cols = pl.ds(pl.multiple_of(z * ZCOL, 128), ZCOL)
            acc_gu[rows, :] += nt(xs[rows, cols], w2[:, cols])

            @pl.when(j == 3)
            def _():
                @pl.loop(0, HALF // 32)
                def _(b):
                    part_rows = pl.ds(pl.multiple_of(h * HALF + b * 32, 16), 32)
                    gate = acc_gu[part_rows, pl.ds(0, HPAD)]
                    upper = acc_gu[part_rows, pl.ds(HPAD, HPAD)]
                    sig = jax.nn.sigmoid(gate)
                    swished = gate * sig
                    hidden[part_rows, :] = (swished * upper).astype(jnp.bfloat16)
                    acc_gu[part_rows, pl.ds(0, HPAD)] = upper * sig * (1.0 + gate * (1.0 - sig))
                    acc_gu[part_rows, pl.ds(HPAD, HPAD)] = swished

        @pl.when(s > 2)
        def _():
            s_chunk(s - 3)

    for h in (0, 1):
        hidden_t[:, pl.ds(h * SIDE, SIDE)] = nn(hidden[pl.ds(h * HALF, HALF), :].T, perm[...]).astype(jnp.bfloat16)
    s_chunk(6)
    s_chunk(7)

    def finish_half(h):
        grad = acc_h[pl.ds(pl.multiple_of(h * SIDE, 16), SIDE), :]
        high = grad.astype(jnp.bfloat16)
        low = (grad - high.astype(jnp.float32)).astype(jnp.bfloat16)
        grad_x[...] = nn(perm[...], high) + nn(perm[...], low)

        @pl.loop(0, HALF // 32)
        def _(b):
            part_rows = pl.ds(pl.multiple_of(h * HALF + b * 32, 16), 32)
            grad = grad_x[pl.ds(pl.multiple_of(b * 32, 16), 32), :]
            hid[part_rows, pl.ds(0, HPAD)] = (grad * acc_gu[part_rows, pl.ds(0, HPAD)]).astype(jnp.bfloat16)
            hid[part_rows, pl.ds(HPAD, HPAD)] = (grad * acc_gu[part_rows, pl.ds(HPAD, HPAD)]).astype(jnp.bfloat16)
            total = jnp.sum(hidden[part_rows, :].astype(jnp.float32) * grad, axis=1, keepdims=True)
            prob[part_rows, :] = jnp.broadcast_to(total, (32, 128))

    def p_y(j):
        return remote(pbuf, py.at[j - 1], p_send.at[j - 1], p_recv.at[j - 1], at_y(j))

    def p_z(j):
        return remote(pz.at[3], pz.at[j - 1], p_send.at[2 + j], p_recv.at[2 + j], at_z(lax.rem(zl + j, 4)))

    def p_b(step):
        return remote(ptot, back.at[rank], pb_send.at[step], pb_recv.at[rank],
                      (d, lax.rem(e + step, 16)))

    def rs_step(n):
        i, q = n // 4, lax.rem(n, 4)
        return lax.rem(zh + 1 + i, 2), lax.rem(zl + 1 + q, 4)

    def piece(yy, n, lo, rows):
        h, z = rs_step(n)
        return (pl.ds(pl.multiple_of(h * HALF + lax.rem(yy, 2) * QTR + lo, 16), rows),
                pl.ds(pl.multiple_of(z * ZCOL + yy // 2 * BLK, 128), BLK))

    def diag_copy(n, way):
        lo, rows = CUT[way]
        return remote(part.at[piece(across, n, lo, rows)], diag.at[n, pl.ds(lo, rows)],
                      rd_send.at[n, way], rd_recv.at[n, way], at_y(turn(n, way)))

    def own_copy(n, way):
        lo, rows = CUT[1 - way]
        to = lax.rem(y + turn(n, way), 4)
        return remote(part.at[piece(to, n, lo, rows)], ybuf.at[n, way, pl.ds(lo, rows)],
                      ro_send.at[n, way], ro_recv.at[n, way], at_y(turn(n, way)))

    def sum_copy(n, way):
        lo, rows = CUT[way]
        return remote(dsum.at[n, pl.ds(lo, rows)], ybuf.at[n, way, pl.ds(lo, rows)],
                      rs_send.at[n, way], rs_recv.at[n, way], at_y(turn(n, way)))

    def zred_copy(n):
        return remote(zsend.at[n], zrecv.at[n], rz_send.at[n], rz_recv.at[n], at_z(rs_step(n)[1]))

    def make_part(n):
        h, z = rs_step(n)
        rows = pl.ds(pl.multiple_of(h * HALF, 16), HALF)
        cols = pl.ds(pl.multiple_of(z * ZCOL, 128), ZCOL)
        part[rows, cols] = nn(hid[rows, :], w2[:, cols]).astype(jnp.bfloat16)
        for way in (0, 1):
            diag_copy(n, way).start()
        for way in (0, 1):
            own_copy(n, way).start()

    def out_copies(q):
        cols = pl.ds(pl.multiple_of(q * ZCOL, 128), ZCOL)
        return (
            pltpu.make_async_copy(ogu.at[pl.ds(0, HID), cols], gg_out.at[:, cols], out_sem.at[q, 0]),
            pltpu.make_async_copy(ogu.at[pl.ds(HPAD, HID), cols], gu_out.at[:, cols], out_sem.at[q, 1]),
            pltpu.make_async_copy(ogd.at[pl.ds(0, HID), cols], gd_out.at[:, cols], out_sem.at[q, 2]),
        )

    def weight_grads(q):
        cols = pl.ds(pl.multiple_of(q * ZCOL, 128), ZCOL)
        ogu[:, cols] = nn(hid_t[...], xs[:, cols]).astype(jnp.bfloat16)
        ogd[:, cols] = nn(hidden_t[...], ss[:, cols]).astype(jnp.bfloat16)
        for out in out_copies(q):
            out.start()

    def y_sum(n):
        for way in (0, 1):
            own_copy(n, way).wait_recv()
            sum_copy(n, way).wait_recv()
        own = part[piece(y, n, 0, QTR)].astype(jnp.float32)
        return own + (ybuf[n, 0].astype(jnp.float32) + ybuf[n, 1].astype(jnp.float32))

    def ret_rank(i, k):
        return lax.rem(zh + 1 + i, 2) * 8 + par * 4 + k

    def ret_copy(i, k, member):
        return remote(retsend.at[i * 4 + k, :, pl.ds(member * 128, WIDE)], retrecv.at[rank],
                      ret_send.at[i * 4 + k, member], ret_recv.at[rank],
                      (d - par + member, expert_of(ret_rank(i, k))))

    def ret_arrival(r):
        return remote(retsend.at[0, :, pl.ds(0, WIDE)], retrecv.at[r], ret_send.at[0, 0], ret_recv.at[r],
                      (d, expert_of(r)))

    def ret_each(i, what):
        for k in range(4):
            for member in (0, 1):
                if i == 0:
                    what(ret_copy(i, k, member))
                else:
                    @pl.when(jnp.logical_or(ret_rank(i, k) != rank, par != member))
                    def _(k=k, member=member):
                        what(ret_copy(i, k, member))

    def send_back(i):
        total = y_sum(i * 4 + 3)
        for q in range(3):
            zred_copy(i * 4 + q).wait_recv()
            total += zrecv[i * 4 + q].astype(jnp.float32)
        slabs = nn(spread[...], total.astype(jnp.bfloat16)).astype(jnp.bfloat16)
        for k in range(4):
            retsend[i * 4 + k] = slabs[k * SLOT : (k + 1) * SLOT]
        ret_each(i, lambda copy: copy.start())
        if i == 1:
            for k in range(4):
                for member in (0, 1):
                    @pl.when(jnp.logical_and(ret_rank(i, k) == rank, par == member))
                    def _(k=k, member=member):
                        retrecv[rank] = slabs[k * SLOT : (k + 1) * SLOT, member * 128 : member * 128 + WIDE]

    finish_half(1 - zh)
    make_part(0)
    make_part(1)
    finish_half(zh)
    for h in (0, 1):
        pbuf[pl.ds(h * 8, 8), :] = jnp.dot(
            row_of[...], prob[pl.ds(h * HALF, HALF), :] * slot_of[...],
            precision=lax.Precision.HIGHEST, preferred_element_type=jnp.float32,
        )

    for j in (1, 2, 3):
        p_y(j).start()
    hid_t[...] = hid[...].T

    @pl.loop(0, 8)
    def _(n):
        @pl.when(n < 6)
        def _():
            make_part(n + 2)

        for way in (0, 1):
            diag_copy(n, way).wait_recv()
            lo, rows = CUT[way]
            to = lax.rem(y + turn(n, way), 4)
            dsum[n, pl.ds(lo, rows)] = (
                part[piece(to, n, lo, rows)].astype(jnp.float32)
                + diag[n, pl.ds(lo, rows)].astype(jnp.float32)
            ).astype(jnp.bfloat16)
            sum_copy(n, way).start()

        @pl.when(n < 4)
        def _():
            weight_grads(n)

        @pl.when(n == 1)
        def _():
            for j in (1, 2, 3):
                p_y(j).wait_recv()
            pz[3] = pbuf[...] + py[0] + py[1] + py[2]
            for j in (1, 2, 3):
                p_z(j).start()

        @pl.when(n == 3)
        def _():
            for j in (1, 2, 3):
                p_z(j).wait_recv()
            ptot[...] = pz[0] + pz[1] + pz[2] + pz[3]
            back[rank] = ptot[...]

            @pl.loop(1, 16)
            def _(step):
                p_b(step).start()

        @pl.when(jnp.logical_and(n > 0, n != 4))
        def _():
            zsend[n - 1] = y_sum(n - 1).astype(jnp.bfloat16)
            zred_copy(n - 1).start()

        @pl.when(n == 4)
        def _():
            send_back(0)

    send_back(1)

    @pl.loop(0, 16)
    def _(r):
        @pl.when(r != rank)
        def _():
            remote(ptot, back.at[r], pb_send.at[0], pb_recv.at[r], (d, expert_of(r))).wait_recv()

    own = jnp.concatenate([back[r, pl.ds(rank, 1), :] for r in range(16)], axis=0)
    own_t = jnp.concatenate([own, jnp.zeros((112, 128), jnp.float32)], axis=0).T
    per_expert = jnp.concatenate(
        [
            jnp.sum(pick[pl.ds(r * SLOT, SLOT), :].astype(jnp.float32) * own_t[:SLOT, r : r + 1],
                    axis=0, keepdims=True)
            for r in range(16)
        ],
        axis=0,
    )
    grads = [
        jnp.sum(jnp.where(ids[pl.ds(k, 1), :] == expert, per_expert, 0.0), axis=0, keepdims=True)
        for k in range(4)
    ]
    droute[...] = (jnp.concatenate(grads, axis=0) / wts[...].astype(jnp.float32)).astype(jnp.bfloat16)

    def from_half(h):
        @pl.loop(0, 8)
        def _(k):
            @pl.when(jnp.logical_or(h * 8 + k != rank, c != par))
            def _():
                ret_arrival(h * 8 + k).wait_recv()

        return nn(pick_t[h], retrecv[pl.ds(h * 8, 8)].reshape(8 * SLOT, WIDE))

    total = from_half(1 - zh)
    total += from_half(zh)
    res[...] = total.T
    dv[...] = (res[pl.ds(pl.multiple_of(par * (WIDE - SHARE), 16), SHARE), :] * factor[...]).astype(jnp.bfloat16)

    @pl.loop(0, 16)
    def _(r):
        @pl.when(jnp.logical_and(r != rank, c == par))
        def _():
            dispatch(r).wait_send()

    for j in (1, 2, 3):
        cot_copy(j).wait_send()
        info_copy(j).wait_send()
    for k in (1, 2, 3, 4):
        for way in (0, 1):
            ring_copy(k, way).wait_send()

    @pl.loop(0, 8)
    def _(o):
        sib_copy(o).wait_send()
        for j in (1, 2, 3):
            sx_copy(o, j).wait_send()

    @pl.loop(1, 16)
    def _(step):
        p_b(step).wait_send()

    for i in (0, 1):
        ret_each(i, lambda copy: copy.wait_send())

    @pl.loop(0, 8)
    def _(s):
        for way in (0, 1):
            y_copy(s, way).wait_send()
            d_copy(s, way).wait_send()
            diag_copy(s, way).wait_send()
            own_copy(s, way).wait_send()
            sum_copy(s, way).wait_send()

    @pl.loop(0, 8)
    def _(s):
        z_each(s // 4, lax.rem(s, 4), lambda copy: copy.wait_send())

    for j in (1, 2, 3):
        p_y(j).wait_send()
        p_z(j).wait_send()

    @pl.loop(0, 4)
    def _(q):
        for out in out_copies(q):
            out.wait()

    for q in range(3):
        zred_copy(q).wait_send()
        zred_copy(4 + q).wait_send()


def finish(dv_in, droute_in, gg_in, gu_in, gd_in, dv, droute, gg, gu, gd, small, tiny, held, in_sem, out_sem):
    trips = [(dv_in, small, dv), (droute_in, tiny, droute)]
    for i, (src, dst) in enumerate(((gg_in, gg), (gu_in, gu), (gd_in, gd))):
        for part in range(3):
            rows = pl.ds(part * 112, 112)
            trips.append((src.at[rows], held.at[i, rows], dst.at[rows]))
    loads = [pltpu.make_async_copy(src, mid, in_sem.at[i]) for i, (src, mid, _) in enumerate(trips)]
    stores = [pltpu.make_async_copy(mid, dst, out_sem.at[i]) for i, (_, mid, dst) in enumerate(trips)]
    for load in loads:
        load.start()
    for load, store in zip(loads, stores):
        load.wait()
        store.start()
    for store in stores:
        store.wait()


def on_device(values, exponents, expert_ids, route_weights, cotangent, w_gate, w_up, w_down):
    vmem, hbm = pl.BlockSpec(memory_space=pltpu.VMEM), pl.BlockSpec(memory_space=pl.ANY)
    dma = pltpu.SemaphoreType.DMA
    bf, f32 = jnp.bfloat16, jnp.float32
    grad = jax.ShapeDtypeStruct((HID, FEAT), bf)
    outs = pl.pallas_call(
        kernel,
        out_shape=(
            jax.ShapeDtypeStruct((SHARE, TOK), bf),
            jax.ShapeDtypeStruct((4, TOK), bf),
            grad, grad, grad,
        ),
        in_specs=[vmem] * 5 + [hbm] * 3,
        out_specs=(vmem, vmem, hbm, hbm, hbm),
        scratch_shapes=[
            pltpu.VMEM((SHARE, TOK), bf),
            pltpu.VMEM((BLK, TOK), bf),
            pltpu.VMEM((SHARE, TOK), f32),
            pltpu.VMEM((16 * SLOT, TOK), bf),
            pltpu.VMEM((2, TOK, 8 * SLOT), bf),
            pltpu.VMEM((2, SIDE, 2 * TOK), bf),
            pltpu.VMEM((QTR, 4 * SLOT), bf),
            pltpu.VMEM((4 * SLOT, QTR), bf),
            pltpu.VMEM((HALF, SIDE), bf),
            pltpu.VMEM((8, HALF), f32),
            pltpu.VMEM((HALF, 128), f32),
            pltpu.VMEM((16, 16, 128), f32),
            pltpu.VMEM((WIDE, TOK), f32),
            pltpu.VMEM((4, 32, TOK), f32),
            pltpu.VMEM((2, FEAT, 2 * TOK), bf),
            pltpu.VMEM((2 * SIDE, FEAT), bf),
            pltpu.VMEM((16, SLOT, BLK), bf),
            pltpu.VMEM((8, SLOT, BLK), bf),
            pltpu.VMEM((ROWS, FEAT), bf),
            pltpu.VMEM((2 * SIDE, FEAT), bf),
            pltpu.VMEM((2 * HPAD, FEAT), bf),
            pltpu.VMEM((HPAD, FEAT), bf),
            pltpu.VMEM((ROWS, 2 * HPAD), f32),
            pltpu.VMEM((2 * SIDE, HPAD), f32),
            pltpu.VMEM((HALF, HPAD), f32),
            pltpu.VMEM((ROWS, 2 * HPAD), bf),
            pltpu.VMEM((ROWS, HPAD), bf),
            pltpu.VMEM((2 * HPAD, ROWS), bf),
            pltpu.VMEM((HPAD, 2 * SIDE), bf),
            pltpu.VMEM((ROWS, 128), f32),
            pltpu.VMEM((ROWS, FEAT), bf),
            pltpu.VMEM((8, QTR, BLK), bf),
            pltpu.VMEM((8, QTR, BLK), bf),
            pltpu.VMEM((8, 2, QTR, BLK), bf),
            pltpu.VMEM((8, QTR, BLK), bf),
            pltpu.VMEM((8, QTR, BLK), bf),
            pltpu.VMEM((8, SLOT, BLK), bf),
            pltpu.VMEM((16, SLOT, WIDE), bf),
            pltpu.VMEM((16, 128), f32),
            pltpu.VMEM((3, 16, 128), f32),
            pltpu.VMEM((4, 16, 128), f32),
            pltpu.VMEM((16, 128), f32),
            pltpu.VMEM((2 * HPAD, FEAT), bf),
            pltpu.VMEM((HPAD, FEAT), bf),
            dma((2,)), dma((16,)), dma((16,)), dma((3,)),
            dma((8, 2)), dma((8,)), dma((8, 2)), dma((8, 2)), dma((8, 2)), dma((8, 2)),
            dma((3,)), dma((3,)), dma((3,)), dma((3,)), dma((2, 4)), dma((2, 4)), dma((8,)), dma((8,)),
            dma((8, 3)), dma((8, 3)),
            dma((8, 2)), dma((8, 2)), dma((8, 2)), dma((8, 2)), dma((8, 2)), dma((8, 2)),
            dma((8,)), dma((8,)),
            dma((8, 2)), dma((16,)), dma((6,)), dma((6,)), dma((16,)), dma((16,)),
            dma((4, 3)),
        ],
        compiler_params=pltpu.CompilerParams(
            collective_id=1, has_side_effects=True, vmem_limit_bytes=56 << 20
        ),
        name="moe_backward",
    )(values.T, cotangent.T, exponents.T, expert_ids.T, route_weights.T, w_gate[0], w_up[0], w_down[0])
    dv, droute, gg, gu, gd = pl.pallas_call(
        finish,
        out_shape=[jax.ShapeDtypeStruct(out.shape, bf) for out in outs],
        in_specs=[hbm] * 5,
        out_specs=[hbm] * 5,
        scratch_shapes=[
            pltpu.VMEM((SHARE, TOK), bf),
            pltpu.VMEM((4, TOK), bf),
            pltpu.VMEM((3, HID, FEAT), bf),
            dma((11,)), dma((11,)),
        ],
        cost_estimate=pl.CostEstimate(flops=0, bytes_accessed=12 << 20, transcendentals=0),
        name="finish",
    )(*outs)
    return dv.T, droute.T, gg[None], gu[None], gd[None]


def solution(mesh):
    in_specs = (
        P("expert", "dp"),
        P("expert", None),
        P("expert", None),
        P("expert", None),
        P("expert", "dp"),
        P("expert", "dp", None),
        P("expert", "dp", None),
        P("expert", "dp", None),
    )
    out_specs = (
        P("expert", "dp"),
        P("expert", None),
        P("expert", "dp", None),
        P("expert", "dp", None),
        P("expert", "dp", None),
    )
    return jax.shard_map(
        on_device, mesh=mesh, in_specs=in_specs, out_specs=out_specs, check_vma=False
    )
```
